256 devices in a mesh: dp: 4 (over x), lat: 64 (over z, y, core).
Axes of the slice: x: 4, y: 4, z: 8, core: 2. Of those that a mesh axis runs over, the one named last changes fastest.
Arguments:
- state: float32 [32, 128, 256, 128], P('dp', 'lat'), may hold values from -8 to 8
- forcing: bfloat16 [32, 128, 256, 128], P('dp', 'lat'), may hold values from -6 to 6
- state_cot: float32 [32, 128, 256, 128], P('dp', 'lat'), may hold values from -8 to 8
- mat_master: float32 [327680], P(('dp', 'lat'))
- mat_moment: float32 [327680], P(('dp', 'lat')), may hold values from -0.0012207031 to 0.0012207031
- mat_second: float32 [327680], P(('dp', 'lat')), may hold values from 1.5993163e-07 to 6.397265e-07
- bias_master: float32 [1408], replicated, may hold values from -1.75 to 1.75
- bias_moment: float32 [1408], replicated, may hold values from -0.0012207031 to 0.0012207031
- bias_second: float32 [1408], replicated, may hold values from 1.5993163e-07 to 6.397265e-07
- level_coupling: float32 [128, 128], replicated, may hold values from -0.5 to 0.5
- lat_of_row: int32 [128], replicated, may hold values from 0 to 127, each once
- step_count: int32 [1], replicated, may hold values from 2 to 20
Outputs:
- state_out: float32 [32, 128, 256, 128], P('dp', 'lat')
- state_grad: float32 [32, 128, 256, 128], P('dp', 'lat')
- mat_grad: float32 [327680], P(('dp', 'lat'))
- mat_new: float32 [327680], P(('dp', 'lat'))
- mat_copy: bfloat16 [327680], P(('dp', 'lat'))
- mat_moment_new: float32 [327680], P(('dp', 'lat'))
- mat_second_new: float32 [327680], P(('dp', 'lat'))
- bias_grad: float32 [1408], replicated
- bias_new: float32 [1408], replicated
- bias_moment_new: float32 [1408], replicated
- bias_second_new: float32 [1408], replicated
- grad_norm: float32 [1], replicated
The draws below stay inside these ranges and needn't reach their ends.
Inputs may be any that keep to these rules, and one draw needn't show every extreme that they name: `lat_of_row`: each latitude index names exactly one stored row.
All inputs are finite; a program needn't handle non-finite values.
Results may differ from the reference program's by a relative error of at most 0.0095.
Values may be sent and summed in bfloat16 or wider, within the bound.
A program may use at most 128 MiB of HBM per device.

```python
import math
import jax
import jax.numpy as jnp
from jax import lax

C = 128
F = 128
H = 256
NLAT = 128
NLON = 256
MW = 128
BATCH = 32
NMAT = 327680
NBIAS = 1408


def draw_mat_master(key, part):
    shapes = [(C, C), (C + F, H), (H, H), (H, H), (H, H), (H, C), (C, C)]
    pieces = []
    for number, sizes_pair in enumerate(shapes):
        height = sizes_pair[0]
        breadth = sizes_pair[1]
        sub_key = jax.random.fold_in(key, number + 11)
        pieces.append(jax.random.normal(sub_key, (height * breadth,), jnp.float32) * height ** (-0.5))
    return jnp.concatenate(pieces)


def zonal_wave(key, amplitude):
    amp_key, phase_key = jax.random.split(key)
    row_amp = jax.random.uniform(amp_key, (BATCH, NLAT, 1, C), jnp.float32, -amplitude, amplitude)
    phase = jax.random.uniform(phase_key, (BATCH, 1, 1, C), jnp.float32, -math.pi, math.pi)
    wave_number = MW - 4
    turns = wave_number * jnp.arange(NLON, dtype=jnp.int32) % NLON
    angles = turns.astype(jnp.float32) * (2.0 * math.pi / NLON)
    return row_amp * jnp.cos(angles[None, None, :, None] + phase)


def draw_state(key, part):
    key = jax.random.fold_in(key, 41)
    noise_key, wave_key = jax.random.split(key)
    shape = (BATCH, NLAT, NLON, C)
    noise = jnp.clip(jax.random.normal(noise_key, shape, jnp.float32), -5.0, 5.0)
    return noise + zonal_wave(wave_key, 3.0)


def draw_state_cot(key, part):
    key = jax.random.fold_in(key, 57)
    noise_key, wave_key = jax.random.split(key)
    shape = (BATCH, NLAT, NLON, C)
    noise = jnp.clip(jax.random.normal(noise_key, shape, jnp.float32), -5.0, 5.0)
    return noise + zonal_wave(wave_key, 3.0)


def level_of(key, shape, shards, least, high):
    def one(dim, blocks):
        steps = jax.random.uniform(jax.random.fold_in(jax.random.fold_in(key, 6), dim), (blocks,), jnp.float32, least / len(shards), high / len(shards))
        return jnp.repeat(jnp.exp(steps), shape[dim] // blocks).reshape((-1,) + (1,) * (len(shape) - dim - 1))

    level = one(*shards[0])
    for cut in shards[1:]:
        level = level * one(*cut)
    return level


def scatter_about(key, shape, spread, reach, cuts=(), kind=jnp.bfloat16):
    drawn = jax.random.normal(key, shape, jnp.float32) * spread
    if len(cuts) > 0:
        drawn = level_of(key, shape, cuts, -0.22, 0.18) * drawn
    return jnp.clip(drawn, min=-reach, max=reach).astype(kind)


def setup_inputs(seed: int = 0) -> dict:
    splits = jax.random.split(jax.random.key(seed), 13)
    state = draw_state(jax.random.fold_in(splits[12], 71), 0)
    forcing = scatter_about(splits[1], (BATCH, NLAT, NLON, F), 1.0, 6.0, ((0, 4), (1, 64)))
    state_cot = draw_state_cot(jax.random.fold_in(splits[12], 71), 0)
    mat_master = draw_mat_master(jax.random.fold_in(splits[12], 71), 0)
    mat_moment = scatter_about(splits[4], (NMAT,), ((NMAT + NBIAS) ** -0.5 / 9), 0.0012207031, ((0, 256),), jnp.float32)
    mat_second = jnp.clip(jnp.exp(math.log(6.397265224222792e-07) - 1.3862944 * jax.random.uniform(splits[5], (NMAT,), jnp.float32) ** level_of(splits[5], (NMAT,), ((0, 256),), -0.2, 0.2)), 1.599316306055698e-07, 6.397265224222792e-07)
    bias_master = scatter_about(splits[6], (NBIAS,), 0.3, 1.75, (), jnp.float32)
    bias_moment = scatter_about(splits[7], (NBIAS,), ((NMAT + NBIAS) ** -0.5 / 9), 0.0012207031, (), jnp.float32)
    bias_second = jnp.clip(jnp.exp(jax.random.uniform(splits[8], (NBIAS,), jnp.float32, math.log(1.599316306055698e-07), math.log(6.397265224222792e-07))), 1.599316306055698e-07, 6.397265224222792e-07)
    level_coupling = scatter_about(splits[9], (C, C), C ** -0.5, 0.5, (), jnp.float32)
    lat_of_row = jax.random.permutation(splits[10], NLAT).astype(jnp.int32)
    step_count = jax.random.randint(splits[11], (1,), 2, 21).astype(jnp.int32)
    return {"state": state, "forcing": forcing, "state_cot": state_cot, "mat_master": mat_master, "mat_moment": mat_moment, "mat_second": mat_second, "bias_master": bias_master, "bias_moment": bias_moment, "bias_second": bias_second, "level_coupling": level_coupling, "lat_of_row": lat_of_row, "step_count": step_count}


@jax.custom_vjp
def low(v):
    return lax.optimization_barrier(v.astype(jnp.bfloat16)).astype(jnp.float32)

@jax.custom_vjp
def low_back(v):
    return v

def low_keep(v):
    return (low(v), None)

def low_pass(kept, grad):
    return (grad,)

def back_keep(v):
    return (v, None)

def back_low(kept, grad):
    return (low(grad),)
low.defvjp(low_keep, low_pass)
low_back.defvjp(back_keep, back_low)
beta_one = 0.9
beta_two = 0.95
learn_rate = 0.3
decay_rate = 0.1
adam_eps = 1e-08
clip_norm = 1.0

def unpack(flat):
    shapes = [(C, C), (C + F, H), (H, H), (H, H), (H, H), (H, C), (C, C)]
    pieces = []
    offset = 0
    for height, breadth in shapes:
        pieces.append(flat[offset:offset + height * breadth].reshape(height, breadth))
        offset += height * breadth
    return pieces

def split_bias(vector):
    return jnp.split(vector, [C, C + H, C + 2 * H, C + 3 * H, C + 4 * H, 2 * C + 4 * H])

def legendre_table(wavenumber, sine_lat, cosine_lat, total_waves):
    k_values = jnp.arange(1, total_waves, dtype=jnp.float32)
    log_terms = jnp.log((2.0 * k_values + 1.0) / (2.0 * k_values))
    below_mask = (k_values[None, :] <= wavenumber[:, None]).astype(jnp.float32)
    log_start = -0.5 * math.log(2.0) + 0.5 * lax.optimization_barrier(jnp.sum(below_mask * log_terms[None, :], axis=1))
    initial = jnp.exp(log_start[:, None] + wavenumber[:, None] * jnp.log(cosine_lat)[None, :])

    def advance(state_pair, offset):
        latest, earlier = state_pair
        degree = wavenumber + offset
        degree_less = degree - 1.0
        factor_up = jnp.sqrt((4.0 * degree * degree - 1.0) / (degree * degree - wavenumber * wavenumber))
        factor_down = jnp.sqrt(jnp.maximum((degree_less * degree_less - wavenumber * wavenumber) / (4.0 * degree_less * degree_less - 1.0), 0.0))
        computed = factor_up[:, None] * (sine_lat[None, :] * latest - factor_down[:, None] * earlier)
        return ((computed, latest), computed)
    offsets = jnp.arange(1, total_waves, dtype=jnp.float32)
    final_pair, stacked = lax.scan(advance, (initial, jnp.zeros_like(initial)), offsets)
    return jnp.concatenate([initial[:, None, :], jnp.moveaxis(stacked, 0, 1)], axis=1)

def grid_tables(slot_ids, total_waves, lon_count):
    live_mask = (slot_ids < total_waves).astype(jnp.float32)
    longitude = jnp.arange(lon_count, dtype=jnp.int32)
    turns = slot_ids[:, None] * longitude[None, :] % lon_count
    angles = turns.astype(jnp.float32) * (2.0 * math.pi / lon_count)
    cosine_vals = jnp.cos(angles)
    sine_vals = jnp.sin(angles)
    forward_scale = live_mask / lon_count
    analysis = jnp.stack([cosine_vals.T * forward_scale[None, :], -sine_vals.T * forward_scale[None, :]], axis=2).reshape(lon_count, -1)
    weight_m = jnp.where(slot_ids == 0, 1.0, 2.0) * live_mask
    synthesis = jnp.stack([cosine_vals * weight_m[:, None], -sine_vals * weight_m[:, None]], axis=1).reshape(-1, lon_count)
    return (analysis, synthesis)

def spectral_tables(wave_ids, lat_of_row, total_waves, nlat_count):
    live_mask = wave_ids < total_waves
    wavenumber = jnp.minimum(wave_ids, total_waves - 1).astype(jnp.float32)
    angles = (lat_of_row.astype(jnp.float32) + 0.5) * (math.pi / nlat_count) - 0.5 * math.pi
    sine_lat = jnp.sin(angles)
    cosine_lat = jnp.cos(angles)
    poly = legendre_table(wavenumber, sine_lat, cosine_lat, total_waves)
    degree = wavenumber[:, None] + jnp.arange(total_waves, dtype=jnp.float32)[None, :]
    valid = (live_mask[:, None] & (degree < total_waves - 0.5)).astype(jnp.float32)
    synth_leg = poly * valid[:, :, None]
    quadrature = math.pi / nlat_count * cosine_lat
    anal_leg = synth_leg * quadrature[None, None, :]
    tendency = degree * (degree + 1.0) / (total_waves * (total_waves - 1.0))
    filt = jnp.exp(-(degree / total_waves) ** 8) * valid
    return (anal_leg, synth_leg, tendency, filt)

def adam_update(weights, moment, second, grads, steps_done):
    moment_new = beta_one * moment + (1.0 - beta_one) * grads
    second_new = beta_two * second + (1.0 - beta_two) * grads * grads
    moment_hat = moment_new / (1.0 - beta_one ** steps_done)
    second_hat = second_new / (1.0 - beta_two ** steps_done)
    weights_new = weights - learn_rate * (moment_hat / (jnp.sqrt(second_hat) + adam_eps) + decay_rate * weights)
    return (weights_new, moment_new, second_new)

def high_dot(left, right):
    return jnp.dot(left, right, precision=lax.Precision.HIGHEST)

def spectral_step(field, tables, coupling):
    analysis, synthesis, anal_leg, synth_leg, tendency, filt = tables
    high = lax.Precision.HIGHEST
    fourier = jnp.einsum('jic,ik->jkc', field, analysis, precision=high).reshape(NLAT, MW, 2, C)
    coef = jnp.einsum('mnj,jmqc->mnqc', anal_leg, fourier, precision=high)
    mixed = jnp.einsum('mnqc,cd->mnqd', coef, coupling, precision=high)
    coef_new = filt[:, :, None, None] * (coef - tendency[:, :, None, None] * mixed)
    back_lat = jnp.einsum('mnj,mnqc->jmqc', synth_leg, coef_new, precision=high).reshape(NLAT, 2 * MW, C)
    return jnp.einsum('jkc,ki->jic', back_lat, synthesis, precision=high)

def column_forward(state_in, flat_in, bias_in, forcing_in, coupling, tables):
    mats = unpack(low(flat_in))
    biases = split_bias(bias_in)
    rows_in = state_in.reshape(-1, C)
    encoded = rows_in + low_back(high_dot(low(rows_in), mats[0])) + biases[0]
    dynamic = spectral_step(encoded.reshape(NLAT, NLON, C), tables, coupling).reshape(-1, C)
    hidden = jnp.concatenate([low(dynamic), forcing_in.reshape(-1, F)], axis=1)
    for layer_id in range(4):
        pre_act = low_back(high_dot(hidden, mats[1 + layer_id])) + biases[1 + layer_id]
        hidden = low(jax.nn.gelu(pre_act))
    middle = dynamic + low_back(high_dot(hidden, mats[5])) + biases[5]
    output = middle + low_back(high_dot(low(middle), mats[6])) + biases[6]
    return output.reshape(NLAT, NLON, C)

def reference(state, forcing, state_cot, mat_master, mat_moment, mat_second, bias_master, bias_moment, bias_second, level_coupling, lat_of_row, step_count):
    wave_ids = jnp.arange(MW, dtype=jnp.int32)
    analysis, synthesis = grid_tables(wave_ids, MW, NLON)
    tables = (analysis, synthesis) + spectral_tables(wave_ids, lat_of_row, MW, NLAT)

    def per_globe(totals, inputs_now):
        state_now, forcing_now, cot_now = inputs_now
        forcing_f = forcing_now.astype(jnp.float32)

        def forward(state_in, flat_in, bias_in):
            return column_forward(state_in, flat_in, bias_in, forcing_f, level_coupling, tables)
        output, pullback = jax.vjp(forward, state_now, mat_master, bias_master)
        back_state, back_flat, back_bias = pullback(cot_now)
        return ((totals[0] + back_flat, totals[1] + back_bias), (output, back_state))
    start_totals = (jnp.zeros(mat_master.shape, jnp.float32), jnp.zeros(bias_master.shape, jnp.float32))
    totals, results = lax.scan(per_globe, start_totals, (state, forcing, state_cot))
    grad_norm = jnp.sqrt(jnp.sum(totals[0] * totals[0]) + jnp.sum(totals[1] * totals[1]))
    clip_factor = jnp.minimum(1.0, clip_norm / (grad_norm + 1e-06))
    mat_grad = totals[0] * clip_factor
    bias_grad = totals[1] * clip_factor
    steps_done = step_count[0].astype(jnp.float32)
    mat_new, mat_moment_new, mat_second_new = adam_update(mat_master, mat_moment, mat_second, mat_grad, steps_done)
    bias_new, bias_moment_new, bias_second_new = adam_update(bias_master, bias_moment, bias_second, bias_grad, steps_done)
    return (results[0], results[1], mat_grad, mat_new, mat_new.astype(jnp.bfloat16), mat_moment_new, mat_second_new, bias_grad, bias_new, bias_moment_new, bias_second_new, grad_norm.reshape(1))
```

```python
import functools
import math

import jax
import jax.numpy as jnp
import ml_dtypes
import numpy as np
from jax import lax
from jax.experimental import pallas as pl
from jax.experimental.pallas import tpu as pltpu
from jax.sharding import PartitionSpec as P

C = 128
F = 128
H = 256
NLAT = 128
NLON = 256
MW = 128
CH = 4
LATS = 64
XS = 4
BIAS_ROWS = 11

beta_one = 0.9
beta_two = 0.95
learn_rate = 0.3
decay_rate = 0.1
adam_eps = 1e-08
clip_norm = 1.0

MESH = pl.DeviceIdType.MESH
f32 = jnp.float32
bf16 = jnp.bfloat16


def zonal_tables():
    wave = np.arange(MW)
    turns = wave[:, None] * np.arange(NLON)[None, :] % NLON
    angle = turns * (2.0 * np.pi / NLON)
    rows = np.stack([np.cos(angle), -np.sin(angle)], axis=1).reshape(2 * MW, NLON)
    swapped = rows.reshape(MW // 4, 2, 4, NLON)[:, ::-1].reshape(2 * MW, NLON)
    both = np.stack([rows, swapped])
    turned = np.swapaxes(both, 1, 2)
    return both.astype(ml_dtypes.bfloat16), turned.astype(ml_dtypes.bfloat16)


def dot(left, right):
    return jnp.dot(left, right, preferred_element_type=f32)


def dot_nt(left, right):
    return lax.dot_general(left, right, (((1,), (1,)), ((), ())), preferred_element_type=f32)


def dot_tn(left, right):
    return lax.dot_general(left, right, (((0,), (0,)), ((), ())), preferred_element_type=f32)


def halves(value):
    top = value.astype(bf16)
    return top, (value - top.astype(f32)).astype(bf16)


def kernel(
    x_hbm,
    frc_hbm,
    cot_hbm,
    wsh_hbm,
    small_hbm,
    lc_hbm,
    bk_hbm,
    bi_hbm,
    so_hbm,
    sg_hbm,
    blk_hbm,
    fin_hbm,
    xv,
    fv,
    cv,
    ov,
    gv,
    wsh,
    small,
    lc,
    bk,
    bi,
    s1,
    r1,
    s2,
    r2,
    s3,
    r3,
    s4,
    r4,
    lq,
    lp,
    lqt,
    lpt,
    cx,
    pex,
    fac,
    fil,
    kap,
    qs,
    wg,
    wflat,
    we,
    ww,
    w5,
    wd,
    lch,
    ff,
    hid,
    gel,
    dwe,
    dww,
    dw5,
    dwd,
    db,
    gf,
    rx,
    s1r,
    rp,
    s2r,
    rq,
    blk,
    pps,
    ppr,
    px,
    pxr,
    pz,
    pzr,
    tot,
    pgr,
    fin,
    xsem,
    isem,
    osem,
    ssem,
    rsem,
    gs,
    gr,
):
    xme = lax.axis_index("dp")
    me = lax.axis_index("lat")
    zme = lax.div(me, 8)
    bme = lax.rem(me, 8)
    odd = lax.rem(me, 2)

    def x_copy(ch):
        part = pl.ds(2 * ch, 2)
        return pltpu.make_async_copy(x_hbm.at[part], xv.at[part], xsem.at[ch])

    loads = [
        pltpu.make_async_copy(bk_hbm, bk, isem.at[0]),
        pltpu.make_async_copy(wsh_hbm, wsh, isem.at[1]),
        pltpu.make_async_copy(small_hbm, small, isem.at[2]),
        pltpu.make_async_copy(lc_hbm, lc, isem.at[3]),
        pltpu.make_async_copy(bi_hbm, bi, isem.at[4]),
        pltpu.make_async_copy(frc_hbm, fv, isem.at[5]),
        pltpu.make_async_copy(cot_hbm, cv, isem.at[6]),
    ]
    loads[0].start()
    for ch in range(CH):
        x_copy(ch).start()
    for load in loads[1:]:
        load.start()

    barrier = pltpu.get_barrier_semaphore()

    def greet(step, carry):
        pl.semaphore_signal(
            barrier, inc=1, device_id={"lat": lax.rem(me + step, LATS)}, device_id_type=MESH
        )
        return carry

    lax.fori_loop(1, LATS, greet, 0)
    for step in range(1, XS):
        pl.semaphore_signal(
            barrier, inc=1, device_id={"dp": lax.rem(xme + step, XS)}, device_id_type=MESH
        )

    sub8 = lax.broadcasted_iota(jnp.int32, (LATS // 2, 8, 128), 1)
    lower = sub8 < 4

    def lat_copy(src, dst, send, recv, peer):
        return pltpu.make_async_remote_copy(
            src_ref=src,
            dst_ref=dst,
            send_sem=send,
            recv_sem=recv,
            device_id={"lat": peer},
            device_id_type=MESH,
        )

    def dp_copy(src, dst, send, recv, peer):
        return pltpu.make_async_remote_copy(
            src_ref=src,
            dst_ref=dst,
            send_sem=send,
            recv_sem=recv,
            device_id={"dp": peer},
            device_id_type=MESH,
        )

    def drain(ref, sem):
        pltpu.make_async_copy(ref, ref, sem).wait()

    def exchange(phase, src, dst, ch):
        def one(step, carry):
            peer = lax.rem(me + step, LATS)
            lat_copy(
                src.at[ch, peer], dst.at[ch, me], ssem.at[phase, ch], rsem.at[phase, ch], peer
            ).start()
            return carry

        lax.fori_loop(1, LATS, one, 0)
        dst[ch, me] = src[ch, me]

    def arrived(phase, dst, ch):
        drain(dst.at[ch, pl.ds(0, LATS - 1)], rsem.at[phase, ch])

    def to_plane(src_of, dst, number):
        for step in range(1, 8):
            other = lax.rem(bme + step, 8)
            lat_copy(src_of(other), dst, gs.at[number], gr.at[number], zme * 8 + other).start()

    def to_column(src, dst, number):
        for step in range(1, 8):
            other = lax.rem(zme + step, 8)
            lat_copy(src, dst, gs.at[number], gr.at[number], other * 8 + bme).start()

    def to_line(src_of, dst, number):
        for step in range(1, XS):
            other = lax.rem(xme + step, XS)
            dp_copy(src_of(other), dst, gs.at[number], gr.at[number], other).start()

    def pack(first, second):
        evens = []
        odds = []
        for globe in range(2):
            lanes = slice(globe * 128, globe * 128 + 128)
            plain = first[:, lanes].reshape(LATS // 2, 8, 128)
            turned = second[:, lanes].reshape(LATS // 2, 8, 128)
            evens.append(jnp.where(lower, plain, turned))
            odds.append(jnp.where(lower, turned, plain))
        even = jnp.concatenate(evens, axis=1).astype(bf16)
        other = jnp.concatenate(odds, axis=1).astype(bf16)
        return jnp.stack([even, other], axis=1).reshape(LATS, 16, 128)

    def unpack(tiles, row):
        pairs = tiles.astype(f32).reshape(LATS // 2, 2, 16, 128)
        straight = jnp.where(row == 0, 1, 0)
        pick = jnp.where(lower, 1, 0) == straight
        sides = []
        for globe in range(2):
            even = pairs[:, 0, globe * 8 : globe * 8 + 8]
            other = pairs[:, 1, globe * 8 : globe * 8 + 8]
            sides.append(jnp.where(pick, even, other).reshape(2 * MW, 128))
        return jnp.concatenate(sides, axis=1).astype(bf16)

    loads[0].wait()

    def analyse(ch, carry):
        x_copy(ch).wait()
        found = []
        for row in range(2):
            sides = jnp.concatenate([xv[2 * ch, row], xv[2 * ch + 1, row]], axis=1)
            found.append(dot(bk[row], sides.astype(bf16)))
        s1[ch] = pack(found[0], found[1])

        @pl.when(ch == 0)
        def _():
            loads[1].wait()
            wg[xme, zme, bme] = wsh[...]
            pl.semaphore_wait(barrier, LATS - 1 + XS - 1)
            to_column(wsh, wg.at[xme, zme, bme], 0)

        @pl.when(ch == 1)
        def _():
            drain(wg.at[0, pl.ds(0, 7), 0], gr.at[0])
            to_plane(lambda other: wg.at[xme, :, bme], wg.at[xme, :, bme], 1)

        @pl.when(ch == 2)
        def _():
            drain(wg.at[0, :, pl.ds(0, 7)], gr.at[1])
            to_line(lambda other: wg.at[xme], wg.at[xme], 2)

        exchange(0, s1, r1, ch)
        return carry

    lax.fori_loop(0, CH, analyse, 0)

    for load in loads[2:5]:
        load.wait()
    lane_col = lax.broadcasted_iota(jnp.int32, (128, 1024), 1)
    lat_index = lax.broadcasted_iota(jnp.int32, (128, 1024), 0)
    row_bit = lax.rem(lax.rem(lax.div(lane_col, 4), 2) + odd, 2)
    one_hot = jnp.where(lat_index == 2 * lax.div(lane_col, 16) + row_bit, 1.0, 0.0).astype(bf16)
    lat = dot(small[16:24, :].astype(bf16), one_hot)[0:1, :]
    phi = (lat + 0.5) * (math.pi / NLAT) - 0.5 * math.pi
    mu = jnp.sin(phi)
    cos_phi = jnp.cos(phi)

    sub = lax.broadcasted_iota(jnp.int32, (128, 128), 0)
    lane = lax.broadcasted_iota(jnp.int32, (128, 128), 1)
    m_zero = 2 * me
    k_safe = jnp.maximum(sub, 1).astype(f32)
    logs = jnp.log((2.0 * k_safe + 1.0) / (2.0 * k_safe))
    starts = []
    for slot in range(2):
        below = (sub >= 1) & (sub <= m_zero + slot)
        starts.append(
            -0.5 * math.log(2.0) + 0.5 * jnp.sum(jnp.where(below, logs, 0.0), axis=0, keepdims=True)
        )
    slot_lane = lax.rem(lax.div(lane, 2), 2)
    start = jnp.where(slot_lane[0:1] == 0, starts[0], starts[1])
    start = jnp.concatenate([start] * 8, axis=1)
    m_lane = (m_zero + slot_lane).astype(f32)
    m_wide = jnp.concatenate([m_lane[0:1]] * 8, axis=1)
    first = jnp.exp(start + m_wide * jnp.log(cos_phi))
    degree = m_lane + sub.astype(f32)
    less = degree - 1.0
    m_square = m_lane * m_lane
    gap = jnp.where(sub == 0, 1.0, degree * degree - m_square)
    fac[0] = jnp.sqrt(jnp.maximum((4.0 * degree * degree - 1.0) / gap, 0.0))
    fac[1] = jnp.sqrt(jnp.maximum((less * less - m_square) / (4.0 * less * less - 1.0), 0.0))
    pex[0:1, :] = first

    def advance(n, pair):
        latest, earlier = pair
        up = jnp.concatenate([fac[0, pl.ds(n, 1), :]] * 8, axis=1)
        down = jnp.concatenate([fac[1, pl.ds(n, 1), :]] * 8, axis=1)
        now = up * (mu * latest - down * earlier)
        pex[pl.ds(n, 1), :] = now
        return (now, latest)

    lax.fori_loop(1, MW, advance, (first, jnp.zeros_like(first)))

    for slot in range(2):
        deg = (m_zero + slot + sub).astype(f32)
        live = deg < MW - 0.5
        ratio = deg / MW
        ratio = ratio * ratio
        ratio = ratio * ratio
        fil[slot] = jnp.where(live, jnp.exp(-(ratio * ratio)), 0.0)
        kap[slot] = deg * (deg + 1.0) / (MW * (MW - 1.0))

    n_wide = lax.broadcasted_iota(jnp.int32, (128, 1024), 0)
    keep = n_wide.astype(f32) + m_wide < MW - 0.5
    weight = jnp.where(m_wide == 0.0, 1.0, 2.0)
    poly = jnp.where(keep, pex[...], 0.0)
    synth = poly * weight
    quad = poly * ((math.pi / NLAT) * cos_phi)
    anal = quad * (1.0 / NLON)
    synth_t = synth.T
    anal_t = anal.T
    lane16 = lax.rem(lane_col[0:1], 16)
    row16 = lax.rem(lax.broadcasted_iota(jnp.int32, (1024, 128), 0), 16)

    def chosen(sixteen, combo):
        return (
            (lax.div(sixteen, 8) == combo // 4)
            & (lax.rem(lax.div(sixteen, 2), 2) == (combo // 2) % 2)
            & (lax.rem(sixteen, 2) == combo % 2)
        )

    for combo in range(8):
        part = slice(combo * 128, combo * 128 + 128)
        mine = chosen(lane16, combo)
        lp[part, :] = jnp.where(mine, synth, 0.0).astype(bf16)
        lq[part, :] = jnp.where(mine, anal, 0.0).astype(bf16)
        mine_t = chosen(row16, combo)
        lpt[:, part] = jnp.where(mine_t, synth_t, 0.0).astype(bf16)
        lqt[:, part] = jnp.where(mine_t, anal_t, 0.0).astype(bf16)
    zero_wave = jnp.sum(jnp.where(chosen(lane16, 0), quad, 0.0), axis=1, keepdims=True)
    zero_wave = jnp.where(me == 0, zero_wave, 0.0)
    qs[...] = jnp.broadcast_to(zero_wave, (128, 128))
    lc_top, lc_low = halves(lc[...])
    lch[0] = lc_top
    lch[1] = lc_low

    drain(wg.at[pl.ds(0, 3)], gr.at[2])

    def spread(group, carry):
        tiles = wg[lax.div(group, 8), lax.rem(group, 8)].astype(f32)
        rows = wflat.at[pl.ds(pl.multiple_of(group * 80, 8), 80)]
        for b in range(8):
            rows[b * 10 : b * 10 + 10, :] = tiles[b, 0:10, :]
        return carry

    lax.fori_loop(0, 32, spread, 0)
    we[...] = wflat[0:128, :].astype(bf16)
    for layer in range(4):
        for side in range(2):
            begin = 128 + 512 * layer + side
            ww[layer, :, side * 128 : side * 128 + 128] = wflat[
                pl.ds(begin, 256, stride=2), :
            ].astype(bf16)
    w5[...] = wflat[2176:2432, :].astype(bf16)
    wd[...] = wflat[2432:2560, :].astype(bf16)
    dwe[...] = jnp.zeros_like(dwe)
    dww[...] = jnp.zeros_like(dww)
    dw5[...] = jnp.zeros_like(dw5)
    dwd[...] = jnp.zeros_like(dwd)
    db[...] = jnp.zeros_like(db)

    def couple(value, transposed):
        top, low = halves(value)
        product = dot_nt if transposed else dot
        return product(top, lch[0]) + product(top, lch[1]) + product(low, lch[0])

    def per_slot(table):
        both = jnp.concatenate([table[0], table[0], table[1], table[1]], axis=0)
        return jnp.concatenate([both, both], axis=0)

    zero_combos = (0, 4)

    def add_zero_wave(value, extra):
        blocks = [value[c * 128 : c * 128 + 128] for c in range(8)]
        for c in zero_combos:
            blocks[c] = blocks[c] + extra
        return jnp.concatenate(blocks, axis=0)

    def dynamics(ch, carry):
        arrived(0, r1, ch)
        coef = dot(lq[...], r1[ch].reshape(1024, 128))
        coef_low = coef.astype(bf16)
        cx[ch] = coef_low
        coef = coef + dot(coef_low, we[...])
        coef = add_zero_wave(coef, qs[...] * small[0:1, :])
        coef = per_slot(fil) * (coef - per_slot(kap) * couple(coef, False))
        s2[ch] = dot(lpt[...], coef.astype(bf16)).astype(bf16).reshape(LATS, 16, 128)
        exchange(1, s2, r2, ch)
        return carry

    lax.fori_loop(0, CH, dynamics, 0)

    loads[5].wait()
    loads[6].wait()
    out_copy = [
        lambda ch: pltpu.make_async_copy(
            ov.at[pl.ds(2 * ch, 2)], so_hbm.at[pl.ds(2 * ch, 2)], osem.at[0, ch]
        ),
        lambda ch: pltpu.make_async_copy(
            gv.at[pl.ds(2 * ch, 2)], sg_hbm.at[pl.ds(2 * ch, 2)], osem.at[1, ch]
        ),
    ]
    c_zero = math.sqrt(2.0 / math.pi)
    c_one = 0.044715

    def bias_row(index, count):
        return jnp.concatenate([small[index + k : index + k + 1, :] for k in range(count)], axis=1)

    def add_bias(index, value):
        total = jnp.sum(value, axis=0, keepdims=True)
        for k in range(value.shape[1] // 128):
            db[index + k : index + k + 1, :] += total[:, k * 128 : k * 128 + 128]

    def two(ref, ch, row):
        return jnp.concatenate([ref[2 * ch, row], ref[2 * ch + 1, row]], axis=0)

    def columns(ch):
        def block(row, carry):
            grid = dot(bi[row], unpack(r2[ch], row))
            dynamic = jnp.concatenate([grid[:, 0:128], grid[:, 128:256]], axis=0)
            hidden = jnp.concatenate([dynamic.astype(bf16), two(fv, ch, row)], axis=1)
            hid[0] = hidden
            for layer in range(4):
                pre = dot(hidden, ww[layer]) + bias_row(1 + 2 * layer, 2)
                square = pre * pre
                inner = pre * (c_zero + (c_zero * c_one) * square)
                bent = jnp.tanh(inner)
                half = 0.5 * pre
                hidden = (half + half * bent).astype(bf16)
                slope = half * (c_zero + (3.0 * c_zero * c_one) * square)
                gel[layer] = (0.5 + 0.5 * bent) + slope * (1.0 - bent * bent)
                hid[layer + 1] = hidden
            middle = dynamic + dot(hidden, w5[...]) + bias_row(9, 1)
            middle_low = middle.astype(bf16)
            output = middle + dot(middle_low, wd[...]) + bias_row(10, 1)
            ov[2 * ch, row] = output[0:256]
            ov[2 * ch + 1, row] = output[256:512]
            upstream = two(cv, ch, row)
            up_low = upstream.astype(bf16)
            dwd[...] += dot_tn(middle_low, up_low)
            add_bias(10, upstream)
            back_mid = upstream + dot_nt(up_low, wd[...])
            mid_low = back_mid.astype(bf16)
            dw5[...] += dot_tn(hidden, mid_low)
            add_bias(9, back_mid)
            back = dot_nt(mid_low, w5[...])
            for layer in (3, 2, 1, 0):
                back_pre = gel[layer] * back
                pre_low = back_pre.astype(bf16)
                dww[layer] += dot_tn(hid[layer], pre_low)
                add_bias(1 + 2 * layer, back_pre)
                if layer > 0:
                    back = dot_nt(pre_low, ww[layer])
                else:
                    back = dot_nt(pre_low, ww[0, 0:128, :])
            back_low = (back_mid + back).astype(bf16)
            sides = jnp.concatenate([back_low[0:256], back_low[256:512]], axis=1)
            ff[row] = dot(bk[row], sides)
            return carry

        lax.fori_loop(0, 2, block, 0)
        out_copy[0](ch).start()
        s3[ch] = pack(ff[0], ff[1])
        exchange(2, s3, r3, ch)

    def adjoint(ch):
        arrived(2, r3, ch)
        back = per_slot(fil) * dot(lp[...], r3[ch].reshape(1024, 128))
        back = back - couple(per_slot(kap) * back, True)
        back_low = back.astype(bf16)
        dwe[...] += dot_tn(cx[ch], back_low)
        flat = qs[...] * (back[0:128] + back[512:640])
        db[0:1, :] += jnp.sum(flat, axis=0, keepdims=True)
        back = back + dot_nt(back_low, we[...])
        s4[ch] = dot(lqt[...], back.astype(bf16)).astype(bf16).reshape(LATS, 16, 128)
        exchange(3, s4, r4, ch)

    def grad_line():
        gf[0:128, :] = jnp.zeros((128, 128), f32)
        for layer in range(4):
            for side in range(2):
                begin = 128 + 512 * layer + side
                gf[pl.ds(begin, 256, stride=2), :] = dww[layer, :, side * 128 : side * 128 + 128]
        gf[2176:2432, :] = dw5[...]
        gf[2432:2560, :] = dwd[...]
        to_line(lambda other: gf.at[pl.ds(pl.multiple_of(other * 640, 8), 640)], rx.at[xme], 3)

    def grad_plane():
        drain(rx.at[pl.ds(0, 3)], gr.at[3])
        total = gf[pl.ds(pl.multiple_of(xme * 640, 8), 640), :]
        for step in range(1, XS):
            total = total + rx[lax.rem(xme + step, XS)]
        s1r[...] = total
        to_plane(lambda other: s1r.at[pl.ds(pl.multiple_of(other * 80, 8), 80)], rp.at[bme], 4)

    def grad_turn():
        drain(rp.at[pl.ds(0, 7)], gr.at[4])
        total = s1r[pl.ds(pl.multiple_of(bme * 80, 8), 80), :]
        for step in range(1, 8):
            total = total + rp[lax.rem(bme + step, 8)]
        s2r[...] = total

        @pl.when(bme == zme)
        def _():
            rq[bme] = s2r[...]

        @pl.when(bme != zme)
        def _():
            lat_copy(s2r, rq.at[zme], gs.at[5], gr.at[5], bme * 8 + zme).start()

    def grad_share():
        @pl.when(bme != zme)
        def _():
            drain(s2r, gr.at[5])

        to_plane(lambda other: rq.at[bme], rq.at[bme], 6)

    def grad_block():
        drain(rq.at[pl.ds(0, 7)], gr.at[6])
        total = rq[0]
        for b in range(1, 8):
            total = total + rq[b]
        blk[...] = total

    def middle_steps(t, carry):
        @pl.when(t < CH)
        def _():
            arrived(1, r2, t)
            columns(t)

        @pl.when(t == CH - 1)
        def _():
            grad_line()

        @pl.when(t >= 2)
        def _():
            adjoint(t - 2)

        @pl.when(t == CH)
        def _():
            grad_plane()

        @pl.when(t == CH + 1)
        def _():
            grad_turn()

        return carry

    lax.fori_loop(0, CH + 2, middle_steps, 0)

    grad_share()
    for b in range(8):
        pps[b, 0:16, :] = dwe[b * 16 : b * 16 + 16, :]
        pps[b, 16:32, :] = db[...]
    to_plane(lambda other: pps.at[other], ppr.at[bme], 7)

    def last_line():
        grad_block()
        drain(ppr.at[pl.ds(0, 7)], gr.at[7])
        total = pps[bme]
        for step in range(1, 8):
            total = total + ppr[lax.rem(bme + step, 8)]
        px[0:32, :] = total
        square = blk[0:8, :] * blk[0:8, :]
        for k in range(1, 10):
            piece = blk[8 * k : 8 * k + 8, :]
            square = square + piece * piece
        px[32:40, :] = square
        to_line(lambda other: px, pxr.at[xme], 8)

    def last_column():
        drain(pxr.at[pl.ds(0, 3)], gr.at[8])
        total = px[...]
        for step in range(1, XS):
            total = total + pxr[lax.rem(xme + step, XS)]
        pz[...] = total
        to_column(pz, pzr.at[zme], 9)

    def last_plane():
        drain(pzr.at[pl.ds(0, 7)], gr.at[9])
        total = pz[...]
        for step in range(1, 8):
            total = total + pzr[lax.rem(zme + step, 8)]
        tot[...] = total
        pgr[bme] = tot[0:16, :]
        to_plane(lambda other: tot.at[pl.ds(0, 16)], pgr.at[bme], 10)

    def finish(ch, carry):
        @pl.when(ch == 1)
        def _():
            last_line()

        @pl.when(ch == 2)
        def _():
            last_column()

        @pl.when(ch == 3)
        def _():
            last_plane()

        arrived(3, r4, ch)
        for row in range(2):
            grid = dot(bi[row], unpack(r4[ch], row))
            gv[2 * ch, row] = grid[:, 0:128]
            gv[2 * ch + 1, row] = grid[:, 128:256]
        out_copy[1](ch).start()
        return carry

    lax.fori_loop(0, CH, finish, 0)

    drain(pgr.at[pl.ds(0, 7)], gr.at[10])
    enc = pgr[...].reshape(128, 128)
    at_zero = jnp.where((xme == 0) & (zme == 0), 1.0, 0.0)
    at_one = jnp.where((xme == 0) & (zme == 1), 1.0, 0.0)
    blk[...] += at_zero * enc[0:80]
    blk[0:48, :] += at_one * enc[80:128]
    bias_total = tot[16:32, :]
    squares = (
        jnp.sum(tot[32:40, :]) + jnp.sum(enc * enc) + jnp.sum(bias_total * bias_total)
    )
    fin[0:16, :] = bias_total
    fin[16:24, :] = jnp.zeros((8, 128), f32) + squares
    last = [
        pltpu.make_async_copy(blk, blk_hbm, isem.at[7]),
        pltpu.make_async_copy(fin, fin_hbm, isem.at[8]),
    ]
    for copy in last:
        copy.start()

    for phase, src in enumerate((s1, s2, s3, s4)):
        for ch in range(CH):
            drain(src.at[ch, pl.ds(0, LATS - 1)], ssem.at[phase, ch])
    drain(wg.at[0, pl.ds(0, 7), 0], gs.at[0])
    drain(wg.at[0, :, pl.ds(0, 7)], gs.at[1])
    drain(wg.at[pl.ds(0, 3)], gs.at[2])
    drain(rx.at[pl.ds(0, 3)], gs.at[3])
    drain(rp.at[pl.ds(0, 7)], gs.at[4])

    @pl.when(bme != zme)
    def _():
        drain(s2r, gs.at[5])

    drain(rq.at[pl.ds(0, 7)], gs.at[6])
    drain(ppr.at[pl.ds(0, 7)], gs.at[7])
    drain(pxr.at[pl.ds(0, 3)], gs.at[8])
    drain(pzr.at[pl.ds(0, 7)], gs.at[9])
    drain(pgr.at[pl.ds(0, 7)], gs.at[10])
    for ch in range(CH):
        out_copy[0](ch).wait()
        out_copy[1](ch).wait()
    for copy in last:
        copy.wait()


def adam_update(weights, moment, second, grads, steps_done):
    moment_new = beta_one * moment + (1.0 - beta_one) * grads
    second_new = beta_two * second + (1.0 - beta_two) * grads * grads
    moment_hat = moment_new / (1.0 - beta_one**steps_done)
    second_hat = second_new / (1.0 - beta_two**steps_done)
    weights_new = weights - learn_rate * (
        moment_hat / (jnp.sqrt(second_hat) + adam_eps) + decay_rate * weights
    )
    return (weights_new, moment_new, second_new)


def local(
    state,
    forcing,
    state_cot,
    mat_master,
    mat_moment,
    mat_second,
    bias_master,
    bias_moment,
    bias_second,
    level_coupling,
    lat_of_row,
    step_count,
):
    wsh = jnp.pad(mat_master.reshape(10, 128), ((0, 6), (0, 0))).astype(bf16)
    small = jnp.concatenate(
        [
            jnp.pad(bias_master.reshape(BIAS_ROWS, 128), ((0, 5), (0, 0))),
            jnp.broadcast_to(lat_of_row.astype(f32)[None, :], (8, 128)),
        ],
        axis=0,
    )
    both, turned = zonal_tables()
    any_spec = pl.BlockSpec(memory_space=pl.ANY)
    big = (8, 2, NLON, C)
    tiles = (CH, LATS, 16, 128)
    vm = pltpu.VMEM
    scratch = [
        vm(big, f32),
        vm(big, bf16),
        vm(big, f32),
        vm(big, f32),
        vm(big, f32),
        vm((16, 128), bf16),
        vm((24, 128), f32),
        vm((128, 128), f32),
        vm((2, 256, 256), bf16),
        vm((2, 256, 256), bf16),
        *[vm(tiles, bf16) for _ in range(8)],
        *[vm((1024, 1024), bf16) for _ in range(4)],
        vm((CH, 1024, 128), bf16),
        vm((128, 1024), f32),
        vm((2, 128, 128), f32),
        vm((2, 128, 128), f32),
        vm((2, 128, 128), f32),
        vm((128, 128), f32),
        vm((XS, 8, 8, 16, 128), bf16),
        vm((2560, 128), f32),
        vm((128, 128), bf16),
        vm((4, 256, 256), bf16),
        vm((256, 128), bf16),
        vm((128, 128), bf16),
        vm((2, 128, 128), bf16),
        vm((2, 256, 256), f32),
        vm((5, 512, 256), bf16),
        vm((4, 512, 256), f32),
        vm((128, 128), f32),
        vm((4, 256, 256), f32),
        vm((256, 128), f32),
        vm((128, 128), f32),
        vm((16, 128), f32),
        vm((2560, 128), f32),
        vm((XS, 640, 128), f32),
        vm((640, 128), f32),
        vm((8, 80, 128), f32),
        vm((80, 128), f32),
        vm((8, 80, 128), f32),
        vm((80, 128), f32),
        vm((8, 32, 128), f32),
        vm((8, 32, 128), f32),
        vm((40, 128), f32),
        vm((XS, 40, 128), f32),
        vm((40, 128), f32),
        vm((8, 40, 128), f32),
        vm((40, 128), f32),
        vm((8, 16, 128), f32),
        vm((24, 128), f32),
        pltpu.SemaphoreType.DMA((CH,)),
        pltpu.SemaphoreType.DMA((9,)),
        pltpu.SemaphoreType.DMA((2, CH)),
        pltpu.SemaphoreType.DMA((4, CH)),
        pltpu.SemaphoreType.DMA((4, CH)),
        pltpu.SemaphoreType.DMA((11,)),
        pltpu.SemaphoreType.DMA((11,)),
    ]
    state_out, state_grad, block, final = pl.pallas_call(
        kernel,
        out_shape=(
            jax.ShapeDtypeStruct(big, f32),
            jax.ShapeDtypeStruct(big, f32),
            jax.ShapeDtypeStruct((80, 128), f32),
            jax.ShapeDtypeStruct((24, 128), f32),
        ),
        in_specs=[any_spec] * 8,
        out_specs=(any_spec,) * 4,
        scratch_shapes=scratch,
        compiler_params=pltpu.CompilerParams(
            collective_id=0, has_side_effects=True, vmem_limit_bytes=60 * 1024 * 1024
        ),
        cost_estimate=pl.CostEstimate(
            flops=16 * 10**9, bytes_accessed=10 * 2**20, transcendentals=4 * 10**6
        ),
        name="column_step",
    )(
        state,
        forcing,
        state_cot,
        wsh,
        small,
        level_coupling,
        jnp.asarray(both),
        jnp.asarray(turned),
    )

    bias_sum = final[0:BIAS_ROWS].reshape(-1)
    grad_norm = jnp.sqrt(final[16, 0])
    clip_factor = jnp.minimum(1.0, clip_norm / (grad_norm + 1e-06))
    place = lax.rem(lax.axis_index("lat"), 8) * 10
    mat_total = lax.dynamic_slice(block, (place, 0), (10, 128)).reshape(-1)
    mat_grad = mat_total * clip_factor
    bias_grad = bias_sum * clip_factor
    steps_done = step_count[0].astype(f32)
    mat_new, mat_moment_new, mat_second_new = adam_update(
        mat_master, mat_moment, mat_second, mat_grad, steps_done
    )
    bias_new, bias_moment_new, bias_second_new = adam_update(
        bias_master, bias_moment, bias_second, bias_grad, steps_done
    )
    return (
        state_out,
        state_grad,
        mat_grad,
        mat_new,
        mat_new.astype(bf16),
        mat_moment_new,
        mat_second_new,
        bias_grad,
        bias_new,
        bias_moment_new,
        bias_second_new,
        grad_norm.reshape(1),
    )


def solution(mesh):
    columns = P("dp", "lat", None, None)
    flat = P(("dp", "lat"))
    return jax.shard_map(
        local,
        mesh=mesh,
        in_specs=(columns,) * 3 + (flat,) * 3 + (P(),) * 6,
        out_specs=(columns,) * 2 + (flat,) * 5 + (P(),) * 5,
        check_vma=False,
    )
```

```python
import functools
import math

import jax
import jax.numpy as jnp
import ml_dtypes
import numpy as np
from jax import lax
from jax.experimental import pallas as pl
from jax.experimental.pallas import tpu as pltpu
from jax.sharding import PartitionSpec as P

C = 128
F = 128
H = 256
NLAT = 128
NLON = 256
MW = 128
CH = 4
LATS = 64
XS = 4
BIAS_ROWS = 11

beta_one = 0.9
beta_two = 0.95
learn_rate = 0.3
decay_rate = 0.1
adam_eps = 1e-08
clip_norm = 1.0

MESH = pl.DeviceIdType.MESH
f32 = jnp.float32
bf16 = jnp.bfloat16


def zonal_tables():
    wave = np.arange(MW)
    turns = wave[:, None] * np.arange(NLON)[None, :] % NLON
    angle = turns * (2.0 * np.pi / NLON)
    rows = np.stack([np.cos(angle), -np.sin(angle)], axis=1).reshape(2 * MW, NLON)
    swapped = rows.reshape(MW // 4, 2, 4, NLON)[:, ::-1].reshape(2 * MW, NLON)
    both = np.stack([rows, swapped])
    turned = np.swapaxes(both, 1, 2)
    return both.astype(ml_dtypes.bfloat16), turned.astype(ml_dtypes.bfloat16)


def dot(left, right):
    return jnp.dot(left, right, preferred_element_type=f32)


def dot_nt(left, right):
    return lax.dot_general(left, right, (((1,), (1,)), ((), ())), preferred_element_type=f32)


def dot_tn(left, right):
    return lax.dot_general(left, right, (((0,), (0,)), ((), ())), preferred_element_type=f32)


def halves(value):
    top = value.astype(bf16)
    return top, (value - top.astype(f32)).astype(bf16)


def kernel(
    x_hbm,
    frc_hbm,
    cot_hbm,
    mat_hbm,
    bias_hbm,
    lat_hbm,
    lc_hbm,
    bk_hbm,
    bi_hbm,
    so_hbm,
    sg_hbm,
    blk_hbm,
    fin_hbm,
    xv,
    fv,
    cv,
    ov,
    gv,
    mat,
    wsh,
    bias,
    lat_in,
    lc,
    bk,
    bi,
    s1,
    r1,
    s2,
    r2,
    s3,
    r3,
    s4,
    r4,
    lq,
    lp,
    lqt,
    lpt,
    rows,
    cx,
    pex,
    fac,
    fil,
    kap,
    qs,
    wz,
    wrow,
    wb,
    wflat,
    we,
    ww,
    w5,
    wd,
    lch,
    ff,
    hid,
    gel,
    dwe,
    dww,
    dw5,
    dwd,
    db,
    gf,
    rk,
    rh,
    rx,
    s1r,
    ry,
    s2r,
    rw,
    blk,
    wide,
    pps,
    ppr,
    px,
    pxr,
    pz,
    pzr,
    pzl,
    pzlr,
    tot,
    pgr,
    fin,
    xsem,
    isem,
    osem,
    ssem,
    rsem,
    gs,
    gr,
):
    xme = lax.axis_index("dp")
    me = lax.axis_index("lat")
    zme = lax.div(me, 8)
    bme = lax.rem(me, 8)
    yme = lax.div(bme, 2)
    odd = lax.rem(me, 2)

    def x_copy(ch):
        part = pl.ds(2 * ch, 2)
        return pltpu.make_async_copy(x_hbm.at[part], xv.at[part], xsem.at[ch])

    loads = [
        pltpu.make_async_copy(bk_hbm, bk, isem.at[0]),
        pltpu.make_async_copy(mat_hbm, mat, isem.at[1]),
        pltpu.make_async_copy(bias_hbm, bias, isem.at[2]),
        pltpu.make_async_copy(lc_hbm, lc, isem.at[3]),
        pltpu.make_async_copy(bi_hbm, bi, isem.at[4]),
        pltpu.make_async_copy(frc_hbm, fv, isem.at[5]),
        pltpu.make_async_copy(cot_hbm, cv, isem.at[6]),
        pltpu.make_async_copy(lat_hbm, lat_in, isem.at[9]),
    ]
    loads[0].start()
    for ch in range(CH):
        x_copy(ch).start()
    for load in loads[1:]:
        load.start()

    barrier = pltpu.get_barrier_semaphore()

    def greet(step, carry):
        pl.semaphore_signal(
            barrier, inc=1, device_id={"lat": lax.rem(me + step, LATS)}, device_id_type=MESH
        )
        return carry

    lax.fori_loop(1, LATS, greet, 0)
    for step in range(1, XS):
        pl.semaphore_signal(
            barrier, inc=1, device_id={"dp": lax.rem(xme + step, XS)}, device_id_type=MESH
        )

    sub8 = lax.broadcasted_iota(jnp.int32, (LATS // 2, 8, 128), 1)
    lower = sub8 < 4

    def lat_copy(src, dst, send, recv, peer):
        return pltpu.make_async_remote_copy(
            src_ref=src,
            dst_ref=dst,
            send_sem=send,
            recv_sem=recv,
            device_id={"lat": peer},
            device_id_type=MESH,
        )

    def dp_copy(src, dst, send, recv, peer):
        return pltpu.make_async_remote_copy(
            src_ref=src,
            dst_ref=dst,
            send_sem=send,
            recv_sem=recv,
            device_id={"dp": peer},
            device_id_type=MESH,
        )

    def drain(ref, sem):
        pltpu.make_async_copy(ref, ref, sem).wait()

    def exchange(phase, src, dst, ch):
        def one(step, carry):
            peer = lax.rem(me + step, LATS)
            lat_copy(
                src.at[ch, peer], dst.at[ch, me], ssem.at[phase, ch], rsem.at[phase, ch], peer
            ).start()
            return carry

        lax.fori_loop(1, LATS, one, 0)
        dst[ch, me] = src[ch, me]

    def arrived(phase, dst, ch):
        drain(dst.at[ch, pl.ds(0, LATS - 1)], rsem.at[phase, ch])

    def to_plane(src_of, dst, number):
        for step in range(1, 8):
            other = lax.rem(bme + step, 8)
            lat_copy(src_of(other), dst, gs.at[number], gr.at[number], zme * 8 + other).start()

    def to_column(src, dst, number):
        for step in range(1, 8):
            other = lax.rem(zme + step, 8)
            lat_copy(src, dst, gs.at[number], gr.at[number], other * 8 + bme).start()

    def to_line(src_of, dst, number):
        for step in range(1, XS):
            other = lax.rem(xme + step, XS)
            dp_copy(src_of(other), dst, gs.at[number], gr.at[number], other).start()

    def pack(first, second):
        evens = []
        odds = []
        for globe in range(2):
            lanes = slice(globe * 128, globe * 128 + 128)
            plain = first[:, lanes].reshape(LATS // 2, 8, 128)
            turned = second[:, lanes].reshape(LATS // 2, 8, 128)
            evens.append(jnp.where(lower, plain, turned))
            odds.append(jnp.where(lower, turned, plain))
        even = jnp.concatenate(evens, axis=1).astype(bf16)
        other = jnp.concatenate(odds, axis=1).astype(bf16)
        return jnp.stack([even, other], axis=1).reshape(LATS, 16, 128)

    def unpack(tiles, row):
        pairs = tiles.astype(f32).reshape(LATS // 2, 2, 16, 128)
        straight = jnp.where(row == 0, 1, 0)
        pick = jnp.where(lower, 1, 0) == straight
        sides = []
        for globe in range(2):
            even = pairs[:, 0, globe * 8 : globe * 8 + 8]
            other = pairs[:, 1, globe * 8 : globe * 8 + 8]
            sides.append(jnp.where(pick, even, other).reshape(2 * MW, 128))
        return jnp.concatenate(sides, axis=1).astype(bf16)

    loads[0].wait()

    def analyse(ch, carry):
        x_copy(ch).wait()
        found = []
        for row in range(2):
            sides = jnp.concatenate([xv[2 * ch, row], xv[2 * ch + 1, row]], axis=1)
            found.append(dot(bk[row], sides.astype(bf16)))
        s1[ch] = pack(found[0], found[1])
        return carry

    lax.fori_loop(0, CH, analyse, 0)

    for number in (1, 2, 3, 7):
        loads[number].wait()
    sub = lax.broadcasted_iota(jnp.int32, (128, 128), 0)
    lane = lax.broadcasted_iota(jnp.int32, (128, 128), 1)
    row_of_lane = 2 * lax.rem(lane, LATS) + lax.rem(lax.div(lane, LATS) + odd, 2)
    one_hot = jnp.where(sub == row_of_lane, 1.0, 0.0).astype(bf16)
    lat_rows = jnp.broadcast_to(lat_in[...].astype(f32), (8, 128)).astype(bf16)
    lat = dot(lat_rows, one_hot)[0:1, :]
    phi = (lat + 0.5) * (math.pi / NLAT) - 0.5 * math.pi
    mu = jnp.sin(phi)
    cos_phi = jnp.cos(phi)
    log_cos = jnp.log(cos_phi)
    m_zero = 2 * me
    k_safe = jnp.maximum(sub, 1).astype(f32)
    logs = jnp.log((2.0 * k_safe + 1.0) / (2.0 * k_safe))
    firsts = []
    for slot in range(2):
        wave = (m_zero + slot).astype(f32)
        below = (sub >= 1) & (sub <= m_zero + slot)
        total = jnp.sum(jnp.where(below, logs, 0.0), axis=0, keepdims=True)
        firsts.append(jnp.exp(-0.5 * math.log(2.0) + 0.5 * total + wave * log_cos))
        pex[slot, 0:1, :] = firsts[slot]
        degree = wave + sub.astype(f32)
        less = degree - 1.0
        square = wave * wave
        gap = jnp.where(sub == 0, 1.0, degree * degree - square)
        fac[slot, 0] = jnp.sqrt(jnp.maximum((4.0 * degree * degree - 1.0) / gap, 0.0))
        fac[slot, 1] = jnp.sqrt(
            jnp.maximum((less * less - square) / (4.0 * less * less - 1.0), 0.0)
        )
        live = degree < MW - 0.5
        ratio = degree / MW
        ratio = ratio * ratio
        ratio = ratio * ratio
        fil[slot] = jnp.where(live, jnp.exp(-(ratio * ratio)), 0.0)
        kap[slot] = degree * (degree + 1.0) / (MW * (MW - 1.0))

    def advance(n, pairs):
        following = []
        for slot in range(2):
            latest, earlier = pairs[slot]
            up = fac[slot, 0, pl.ds(n, 1), :]
            down = fac[slot, 1, pl.ds(n, 1), :]
            now = up * (mu * latest - down * earlier)
            pex[slot, pl.ds(n, 1), :] = now
            following.append((now, latest))
        return tuple(following)

    lax.fori_loop(
        1, MW, advance, tuple((firsts[slot], jnp.zeros((1, 128), f32)) for slot in range(2))
    )

    for slot in range(2):
        keep = m_zero + slot + sub < MW
        poly = jnp.where(keep, pex[slot], 0.0)
        synth = poly * jnp.where(m_zero + slot == 0, 1.0, 2.0)
        quad = poly * ((math.pi / NLAT) * cos_phi)
        anal = quad * (1.0 / NLON)
        lp[slot] = synth.astype(bf16)
        lq[slot] = anal.astype(bf16)
        lpt[slot] = synth.T.astype(bf16)
        lqt[slot] = anal.T.astype(bf16)
        if slot == 0:
            zero_wave = jnp.sum(quad, axis=1, keepdims=True)
            zero_wave = jnp.where(me == 0, zero_wave, 0.0)
            qs[...] = jnp.broadcast_to(zero_wave, (128, 128))
    lc_top, lc_low = halves(lc[...])
    lch[0] = lc_top
    lch[1] = lc_low

    wsh[...] = jnp.concatenate([mat[...], jnp.zeros((6, 128), f32)], axis=0).astype(bf16)
    wz[zme] = wsh[...]
    pl.semaphore_wait(barrier, LATS - 1 + XS - 1)
    to_column(wsh, wz.at[zme], 0)
    exchange(0, s1, r1, 0)
    exchange(0, s1, r1, 1)

    drain(wz.at[pl.ds(0, 7)], gr.at[0])
    tiles = wz[...].astype(f32)
    for z in range(8):
        wrow[z * 10 : z * 10 + 10, :] = tiles[z, 0:10, :]
    wb[xme, bme] = wrow[...].astype(bf16)
    to_plane(lambda other: wb.at[xme, bme], wb.at[xme, bme], 1)
    exchange(0, s1, r1, 2)

    drain(wb.at[0, pl.ds(0, 7)], gr.at[1])
    own_part = wb.at[xme, pl.ds(4 * odd, 4)]
    to_line(lambda other: own_part, own_part, 2)
    exchange(0, s1, r1, 3)

    drain(wb.at[pl.ds(0, 3), pl.ds(0, 4)], gr.at[2])
    for step in range(1, XS):
        part = wb.at[lax.rem(xme + step, XS), pl.ds(4 * odd, 4)]
        lat_copy(part, part, gs.at[11], gr.at[11], me + 1 - 2 * odd).start()

    drain(wb.at[pl.ds(0, 3), pl.ds(0, 4)], gr.at[11])

    def spread(line, carry):
        for b in range(8):
            tile = wb[line, b].astype(f32)
            for z in range(8):
                target = wflat.at[pl.ds(pl.multiple_of(line * 640, 8), 640)]
                begin = z * 80 + b * 10
                target[begin : begin + 10, :] = tile[z * 10 : z * 10 + 10, :]
        return carry

    lax.fori_loop(0, XS, spread, 0)
    we[...] = wflat[0:128, :].astype(bf16)
    for layer in range(4):
        for side in range(2):
            begin = 128 + 512 * layer + side
            ww[layer, :, side * 128 : side * 128 + 128] = wflat[
                pl.ds(begin, 256, stride=2), :
            ].astype(bf16)
    w5[...] = wflat[2176:2432, :].astype(bf16)
    wd[...] = wflat[2432:2560, :].astype(bf16)
    loads[4].wait()
    dwe[...] = jnp.zeros_like(dwe)
    dww[...] = jnp.zeros_like(dww)
    dw5[...] = jnp.zeros_like(dw5)
    dwd[...] = jnp.zeros_like(dwd)
    db[...] = jnp.zeros_like(db)

    def couple(value, transposed):
        top, low = halves(value)
        product = dot_nt if transposed else dot
        return product(top, lch[0]) + product(top, lch[1]) + product(low, lch[0])

    def per_slot(table):
        return jnp.concatenate([table[0]] * 4 + [table[1]] * 4, axis=0)

    def gather_rows(tiles, slot):
        if slot == 0:
            rows[...] = tiles.astype(f32).reshape(1024, 128)
        sides = []
        for globe in range(2):
            for part in range(2):
                begin = globe * 8 + slot * 2 + part
                sides.append(
                    jnp.concatenate(
                        [rows[pl.ds(begin + 4 * k, LATS, stride=16), :] for k in range(2)], axis=0
                    )
                )
        return jnp.concatenate(sides, axis=1).astype(bf16)

    def to_coefficients(table, tiles):
        blocks = []
        for slot in range(2):
            found = dot(table[slot], gather_rows(tiles, slot))
            blocks += [found[:, k * 128 : k * 128 + 128] for k in range(4)]
        return blocks

    def to_tiles(table, blocks):
        for slot in range(2):
            wide_low = jnp.concatenate(blocks[4 * slot : 4 * slot + 4], axis=1).astype(bf16)
            found = dot(table[slot], wide_low)
            for globe in range(2):
                for part in range(2):
                    begin = globe * 8 + slot * 2 + part
                    lanes = slice((globe * 2 + part) * 128, (globe * 2 + part) * 128 + 128)
                    for k in range(2):
                        rows[pl.ds(begin + 4 * k, LATS, stride=16), :] = found[
                            k * LATS : k * LATS + LATS, lanes
                        ]
        return rows[...].astype(bf16).reshape(LATS, 16, 128)

    def cut(value):
        return [value[c * 128 : c * 128 + 128] for c in range(8)]

    def dynamics(ch, carry):
        arrived(0, r1, ch)
        blocks = to_coefficients(lq, r1[ch])
        coef = jnp.concatenate(blocks, axis=0)
        coef_low = coef.astype(bf16)
        cx[ch] = coef_low
        blocks = cut(coef + dot(coef_low, we[...]))
        constant = qs[...] * bias[0:1, :]
        blocks[0] = blocks[0] + constant
        blocks[2] = blocks[2] + constant
        coef = jnp.concatenate(blocks, axis=0)
        coef = per_slot(fil) * (coef - per_slot(kap) * couple(coef, False))
        s2[ch] = to_tiles(lpt, cut(coef))
        exchange(1, s2, r2, ch)
        return carry

    lax.fori_loop(0, CH, dynamics, 0)

    loads[5].wait()
    loads[6].wait()
    out_copy = [
        lambda ch: pltpu.make_async_copy(
            ov.at[pl.ds(2 * ch, 2)], so_hbm.at[pl.ds(2 * ch, 2)], osem.at[0, ch]
        ),
        lambda ch: pltpu.make_async_copy(
            gv.at[pl.ds(2 * ch, 2)], sg_hbm.at[pl.ds(2 * ch, 2)], osem.at[1, ch]
        ),
    ]
    c_zero = math.sqrt(2.0 / math.pi)
    c_one = 0.044715

    def bias_row(index, count):
        return jnp.concatenate([bias[index + k : index + k + 1, :] for k in range(count)], axis=1)

    def add_bias(index, value):
        total = jnp.sum(value, axis=0, keepdims=True)
        for k in range(value.shape[1] // 128):
            db[index + k : index + k + 1, :] += total[:, k * 128 : k * 128 + 128]

    def two(ref, ch, row):
        return jnp.concatenate([ref[2 * ch, row], ref[2 * ch + 1, row]], axis=0)

    def columns(ch):
        def block(row, carry):
            grid = dot(bi[row], unpack(r2[ch], row))
            dynamic = jnp.concatenate([grid[:, 0:128], grid[:, 128:256]], axis=0)
            hidden = jnp.concatenate([dynamic.astype(bf16), two(fv, ch, row)], axis=1)
            hid[0] = hidden
            for layer in range(4):
                pre = dot(hidden, ww[layer]) + bias_row(1 + 2 * layer, 2)
                square = pre * pre
                inner = pre * (c_zero + (c_zero * c_one) * square)
                bent = jnp.tanh(inner)
                half = 0.5 * pre
                hidden = (half + half * bent).astype(bf16)
                slope = half * (c_zero + (3.0 * c_zero * c_one) * square)
                gel[layer] = (0.5 + 0.5 * bent) + slope * (1.0 - bent * bent)
                hid[layer + 1] = hidden
            middle = dynamic + dot(hidden, w5[...]) + bias_row(9, 1)
            middle_low = middle.astype(bf16)
            output = middle + dot(middle_low, wd[...]) + bias_row(10, 1)
            ov[2 * ch, row] = output[0:256]
            ov[2 * ch + 1, row] = output[256:512]
            upstream = two(cv, ch, row)
            up_low = upstream.astype(bf16)
            dwd[...] += dot_tn(middle_low, up_low)
            add_bias(10, upstream)
            back_mid = upstream + dot_nt(up_low, wd[...])
            mid_low = back_mid.astype(bf16)
            dw5[...] += dot_tn(hidden, mid_low)
            add_bias(9, back_mid)
            back = dot_nt(mid_low, w5[...])
            for layer in (3, 2, 1, 0):
                back_pre = gel[layer] * back
                pre_low = back_pre.astype(bf16)
                dww[layer] += dot_tn(hid[layer], pre_low)
                add_bias(1 + 2 * layer, back_pre)
                if layer > 0:
                    back = dot_nt(pre_low, ww[layer])
                else:
                    back = dot_nt(pre_low, ww[0, 0:128, :])
            back_low = (back_mid + back).astype(bf16)
            sides = jnp.concatenate([back_low[0:256], back_low[256:512]], axis=1)
            ff[row] = dot(bk[row], sides)
            return carry

        lax.fori_loop(0, 2, block, 0)
        out_copy[0](ch).start()
        s3[ch] = pack(ff[0], ff[1])
        exchange(2, s3, r3, ch)

    def adjoint(ch):
        arrived(2, r3, ch)
        back = jnp.concatenate(to_coefficients(lp, r3[ch]), axis=0)
        back = per_slot(fil) * back
        back = back - couple(per_slot(kap) * back, True)
        back_low = back.astype(bf16)
        dwe[...] += dot_tn(cx[ch], back_low)
        flat = qs[...] * (back[0:128] + back[256:384])
        db[0:1, :] += jnp.sum(flat, axis=0, keepdims=True)
        back = back + dot_nt(back_low, we[...])
        s4[ch] = to_tiles(lqt, cut(back))

    def grad_core():
        gf[0:128, :] = jnp.zeros((128, 128), f32)
        for layer in range(4):
            for side in range(2):
                begin = 128 + 512 * layer + side
                gf[pl.ds(begin, 256, stride=2), :] = dww[layer, :, side * 128 : side * 128 + 128]
        gf[2176:2432, :] = dw5[...]
        gf[2432:2560, :] = dwd[...]

        def one(part, carry):
            begin = pl.multiple_of(part * 160 + 80 * (1 - odd), 8)
            lat_copy(
                gf.at[pl.ds(begin, 80)], rk.at[part], gs.at[12], gr.at[12], me + 1 - 2 * odd
            ).start()
            return carry

        lax.fori_loop(0, 16, one, 0)

    def grad_line():
        drain(rk, gr.at[12])

        def one(part, carry):
            begin = pl.multiple_of(part * 160 + 80 * odd, 8)
            total = rk[part] + gf[pl.ds(begin, 80), :]
            rk[part] = total
            rh[part] = total.astype(bf16)
            return carry

        lax.fori_loop(0, 16, one, 0)
        to_line(lambda other: rh.at[pl.ds(4 * other, 4)], rx.at[xme], 3)

    def grad_row():
        drain(rx.at[pl.ds(0, 3)], gr.at[3])
        total = rk[pl.ds(4 * xme, 4)]
        for step in range(1, XS):
            total = total + rx[lax.rem(xme + step, XS)].astype(f32)
        s1r[...] = total
        for step in range(1, 4):
            other = lax.rem(yme + step, 4)
            peer = zme * 8 + other * 2 + odd
            lat_copy(s1r.at[other], ry.at[yme], gs.at[4], gr.at[4], peer).start()

    def grad_column():
        drain(ry.at[pl.ds(0, 3)], gr.at[4])
        total = s1r[yme]
        for step in range(1, 4):
            total = total + ry[lax.rem(yme + step, 4)]
        for b in range(8):
            begin = 8 * (10 * b // 8)
            s2r[b] = total[begin : begin + 16].astype(bf16)
        for step in range(8):
            other = lax.rem(bme + step, 8)
            peer = bme * 8 + other

            @pl.when(peer != me)
            def _():
                lat_copy(
                    s2r.at[other], rw.at[zme], gs.at[5], gr.at[5], peer
                ).start()

            @pl.when(peer == me)
            def _():
                rw[zme] = s2r[other]

    def turn_bytes(sem):
        @pl.when(bme == zme)
        def _():
            drain(rw.at[pl.ds(0, 7)], sem)

        @pl.when(bme != zme)
        def _():
            drain(rw, sem)

    def grad_block():
        turn_bytes(gr.at[5])
        total = rw[0].astype(f32)
        for z in range(1, 8):
            total = total + rw[z].astype(f32)
        row = lax.broadcasted_iota(jnp.int32, (16, 128), 0)
        begin = 2 * lax.rem(bme, 4)
        total = jnp.where((row >= begin) & (row < begin + 10), total, 0.0)
        blk[...] = total
        return total * total

    def forward_steps(ch, carry):
        arrived(1, r2, ch)
        columns(ch)
        return carry

    lax.fori_loop(0, CH, forward_steps, 0)
    grad_core()

    def adjoint_steps(ch, carry):
        adjoint(ch)

        @pl.when(ch == 0)
        def _():
            exchange(3, s4, r4, 0)
            grad_line()

        @pl.when(ch == 1)
        def _():
            grad_row()

        @pl.when(ch == 2)
        def _():
            grad_column()

        return carry

    lax.fori_loop(0, CH, adjoint_steps, 0)

    for b in range(8):
        pps[b, 0:16, :] = dwe[b * 16 : b * 16 + 16, :]
        pps[b, 16:32, :] = db[...]
    to_plane(lambda other: pps.at[other], ppr.at[bme], 7)
    exchange(3, s4, r4, 1)

    def last_line():
        drain(ppr.at[pl.ds(0, 7)], gr.at[7])
        total = pps[bme]
        for step in range(1, 8):
            total = total + ppr[lax.rem(bme + step, 8)]
        px[0:32, :] = total
        square = grad_block()
        px[32:40, :] = square[0:8] + square[8:16]
        to_line(lambda other: px, pxr.at[xme], 8)

    def last_column():
        drain(pxr.at[pl.ds(0, 3)], gr.at[8])
        total = px[...]
        for step in range(1, XS):
            total = total + pxr[lax.rem(xme + step, XS)]
        pzl[...] = total[0:16].astype(bf16)
        pz[...] = jnp.zeros((8, 128), f32)
        two_rows = jnp.zeros((2, 128), f32)
        for k in range(8):
            chosen = jnp.where(bme == k, 1.0, 0.0)
            two_rows = two_rows + chosen * total[16 + 2 * k : 18 + 2 * k]
        pz[0:2, :] = two_rows
        pz[2:3, :] = jnp.sum(total[32:40], axis=0, keepdims=True)
        to_column(pz, pzr.at[zme], 9)
        to_column(pzl, pzlr.at[zme], 13)

    def last_plane():
        drain(pzr.at[pl.ds(0, 7)], gr.at[9])
        drain(pzlr.at[pl.ds(0, 7)], gr.at[13])
        total = pz[...]
        wide_total = pzl[...].astype(f32)
        for step in range(1, 8):
            total = total + pzr[lax.rem(zme + step, 8)]
            wide_total = wide_total + pzlr[lax.rem(zme + step, 8)].astype(f32)
        tot[0:16, :] = wide_total
        tot[16:24, :] = total
        pgr[bme] = tot[...]
        to_plane(lambda other: tot, pgr.at[bme], 10)


    def finish(ch, carry):
        arrived(3, r4, ch)
        for row in range(2):
            grid = dot(bi[row], unpack(r4[ch], row))
            gv[2 * ch, row] = grid[:, 0:128]
            gv[2 * ch + 1, row] = grid[:, 128:256]
        out_copy[1](ch).start()

        @pl.when(ch == 0)
        def _():
            exchange(3, s4, r4, 2)
            last_line()
            last_column()

        @pl.when(ch == 1)
        def _():
            exchange(3, s4, r4, 3)

        @pl.when(ch == 2)
        def _():
            last_plane()

        return carry

    lax.fori_loop(0, CH, finish, 0)

    drain(pgr.at[pl.ds(0, 7)], gr.at[10])
    enc = pgr[:, 0:16, :].reshape(128, 128)
    row = lax.broadcasted_iota(jnp.int32, (128, 128), 0)
    first_row = 640 * xme + 10 * me
    wide[0:128, :] = jnp.where((row >= first_row) & (row < first_row + 10), enc, 0.0)
    wide[128:160, :] = jnp.zeros((32, 128), f32)

    @pl.when((xme == 0) & (zme < 2))
    def _():
        begin = pl.multiple_of(80 * zme + 8 * lax.div(10 * bme, 8), 8)
        blk[...] += wide[pl.ds(begin, 16), :]

    for b in range(8):
        fin[2 * b : 2 * b + 2, :] = pgr[b, 16:18, :]
    bias_total = fin[0:16, :]
    squares = (
        jnp.sum(pgr[:, 18, :]) + jnp.sum(enc * enc) + jnp.sum(bias_total * bias_total)
    )
    norm = jnp.sqrt(jnp.zeros((8, 128), f32) + squares)
    clip = jnp.minimum(1.0, clip_norm / (norm + 1e-06))
    both_clip = jnp.concatenate([clip, clip], axis=0)
    fin[0:16, :] = bias_total * both_clip
    fin[16:24, :] = norm
    blk[...] = blk[...] * both_clip
    last = [
        pltpu.make_async_copy(blk, blk_hbm, isem.at[7]),
        pltpu.make_async_copy(fin, fin_hbm, isem.at[8]),
    ]
    for copy in last:
        copy.start()

    for phase, src in enumerate((s1, s2, s3, s4)):
        for ch in range(CH):
            drain(src.at[ch, pl.ds(0, LATS - 1)], ssem.at[phase, ch])
    drain(wz.at[pl.ds(0, 7)], gs.at[0])
    drain(wb.at[0, pl.ds(0, 7)], gs.at[1])
    drain(wb.at[pl.ds(0, 3), pl.ds(0, 4)], gs.at[2])
    drain(wb.at[pl.ds(0, 3), pl.ds(0, 4)], gs.at[11])
    drain(rk, gs.at[12])
    drain(rx.at[pl.ds(0, 3)], gs.at[3])
    drain(ry.at[pl.ds(0, 3)], gs.at[4])

    turn_bytes(gs.at[5])
    drain(ppr.at[pl.ds(0, 7)], gs.at[7])
    drain(pxr.at[pl.ds(0, 3)], gs.at[8])
    drain(pzr.at[pl.ds(0, 7)], gs.at[9])
    drain(pzlr.at[pl.ds(0, 7)], gs.at[13])
    drain(pgr.at[pl.ds(0, 7)], gs.at[10])
    for ch in range(CH):
        out_copy[0](ch).wait()
        out_copy[1](ch).wait()
    for copy in last:
        copy.wait()


def adam_update(weights, moment, second, grads, steps_done):
    moment_new = beta_one * moment + (1.0 - beta_one) * grads
    second_new = beta_two * second + (1.0 - beta_two) * grads * grads
    moment_hat = moment_new / (1.0 - beta_one**steps_done)
    second_hat = second_new / (1.0 - beta_two**steps_done)
    weights_new = weights - learn_rate * (
        moment_hat / (jnp.sqrt(second_hat) + adam_eps) + decay_rate * weights
    )
    return (weights_new, moment_new, second_new)


def local(
    state,
    forcing,
    state_cot,
    mat_master,
    mat_moment,
    mat_second,
    bias_master,
    bias_moment,
    bias_second,
    level_coupling,
    lat_of_row,
    step_count,
):
    both, turned = zonal_tables()
    any_spec = pl.BlockSpec(memory_space=pl.ANY)
    big = (8, 2, NLON, C)
    tiles = (CH, LATS, 16, 128)
    vm = pltpu.VMEM
    scratch = [
        vm(big, f32),
        vm(big, bf16),
        vm(big, f32),
        vm(big, f32),
        vm(big, f32),
        vm((10, 128), f32),
        vm((16, 128), bf16),
        vm((BIAS_ROWS, 128), f32),
        vm((1, 128), jnp.int32),
        vm((128, 128), f32),
        vm((2, 256, 256), bf16),
        vm((2, 256, 256), bf16),
        *[vm(tiles, bf16) for _ in range(8)],
        *[vm((2, 128, 128), bf16) for _ in range(4)],
        vm((1024, 128), f32),
        vm((CH, 1024, 128), bf16),
        vm((2, 128, 128), f32),
        vm((2, 2, 128, 128), f32),
        vm((2, 128, 128), f32),
        vm((2, 128, 128), f32),
        vm((128, 128), f32),
        vm((8, 16, 128), bf16),
        vm((80, 128), f32),
        vm((XS, 8, 80, 128), bf16),
        vm((2560, 128), f32),
        vm((128, 128), bf16),
        vm((4, 256, 256), bf16),
        vm((256, 128), bf16),
        vm((128, 128), bf16),
        vm((2, 128, 128), bf16),
        vm((2, 256, 256), f32),
        vm((5, 512, 256), bf16),
        vm((4, 512, 256), f32),
        vm((128, 128), f32),
        vm((4, 256, 256), f32),
        vm((256, 128), f32),
        vm((128, 128), f32),
        vm((16, 128), f32),
        vm((2560, 128), f32),
        vm((16, 80, 128), f32),
        vm((16, 80, 128), bf16),
        vm((XS, 4, 80, 128), bf16),
        vm((4, 80, 128), f32),
        vm((4, 80, 128), f32),
        vm((8, 16, 128), bf16),
        vm((8, 16, 128), bf16),
        vm((16, 128), f32),
        vm((160, 128), f32),
        vm((8, 32, 128), f32),
        vm((8, 32, 128), f32),
        vm((40, 128), f32),
        vm((XS, 40, 128), f32),
        vm((8, 128), f32),
        vm((8, 8, 128), f32),
        vm((16, 128), bf16),
        vm((8, 16, 128), bf16),
        vm((24, 128), f32),
        vm((8, 24, 128), f32),
        vm((24, 128), f32),
        pltpu.SemaphoreType.DMA((CH,)),
        pltpu.SemaphoreType.DMA((10,)),
        pltpu.SemaphoreType.DMA((2, CH)),
        pltpu.SemaphoreType.DMA((4, CH)),
        pltpu.SemaphoreType.DMA((4, CH)),
        pltpu.SemaphoreType.DMA((14,)),
        pltpu.SemaphoreType.DMA((14,)),
    ]
    state_out, state_grad, block, final = pl.pallas_call(
        kernel,
        out_shape=(
            jax.ShapeDtypeStruct(big, f32),
            jax.ShapeDtypeStruct(big, f32),
            jax.ShapeDtypeStruct((16, 128), f32),
            jax.ShapeDtypeStruct((24, 128), f32),
        ),
        in_specs=[any_spec] * 9,
        out_specs=(any_spec,) * 4,
        scratch_shapes=scratch,
        compiler_params=pltpu.CompilerParams(
            collective_id=0, has_side_effects=True, vmem_limit_bytes=60 * 1024 * 1024
        ),
        cost_estimate=pl.CostEstimate(
            flops=16 * 10**9, bytes_accessed=10 * 2**20, transcendentals=4 * 10**6
        ),
        name="column_step",
    )(
        state,
        forcing,
        state_cot,
        mat_master.reshape(10, 128),
        bias_master.reshape(BIAS_ROWS, 128),
        lat_of_row.reshape(1, 128),
        level_coupling,
        jnp.asarray(both),
        jnp.asarray(turned),
    )

    bias_grad = final[0:BIAS_ROWS].reshape(-1)
    place = 2 * lax.rem(lax.axis_index("lat"), 4)
    mat_grad = lax.dynamic_slice(block, (place, 0), (10, 128)).reshape(-1)
    steps_done = step_count[0].astype(f32)
    mat_new, mat_moment_new, mat_second_new = adam_update(
        mat_master, mat_moment, mat_second, mat_grad, steps_done
    )
    bias_new, bias_moment_new, bias_second_new = adam_update(
        bias_master, bias_moment, bias_second, bias_grad, steps_done
    )
    return (
        state_out,
        state_grad,
        mat_grad,
        mat_new,
        mat_new.astype(bf16),
        mat_moment_new,
        mat_second_new,
        bias_grad,
        bias_new,
        bias_moment_new,
        bias_second_new,
        final[16, 0:1],
    )


def solution(mesh):
    columns = P("dp", "lat", None, None)
    flat = P(("dp", "lat"))
    return jax.shard_map(
        local,
        mesh=mesh,
        in_specs=(columns,) * 3 + (flat,) * 3 + (P(),) * 6,
        out_specs=(columns,) * 2 + (flat,) * 5 + (P(),) * 5,
        check_vma=False,
    )
```

```python
import functools
import math

import jax
import jax.numpy as jnp
import ml_dtypes
import numpy as np
from jax import lax
from jax.experimental import pallas as pl
from jax.experimental.pallas import tpu as pltpu
from jax.sharding import PartitionSpec as P

C = 128
F = 128
H = 256
NLAT = 128
NLON = 256
MW = 128
CH = 4
LATS = 64
XS = 4
BIAS_ROWS = 11

beta_one = 0.9
beta_two = 0.95
learn_rate = 0.3
decay_rate = 0.1
adam_eps = 1e-08
clip_norm = 1.0

MESH = pl.DeviceIdType.MESH
f32 = jnp.float32
bf16 = jnp.bfloat16


def zonal_tables():
    wave = np.arange(MW)
    turns = wave[:, None] * np.arange(NLON)[None, :] % NLON
    angle = turns * (2.0 * np.pi / NLON)
    rows = np.stack([np.cos(angle), -np.sin(angle)], axis=1).reshape(2 * MW, NLON)
    swapped = rows.reshape(MW // 4, 2, 4, NLON)[:, ::-1].reshape(2 * MW, NLON)
    both = np.stack([rows, swapped])
    turned = np.swapaxes(both, 1, 2)
    return both.astype(ml_dtypes.bfloat16), turned.astype(ml_dtypes.bfloat16)


def dot(left, right):
    return jnp.dot(left, right, preferred_element_type=f32)


def dot_nt(left, right):
    return lax.dot_general(left, right, (((1,), (1,)), ((), ())), preferred_element_type=f32)


def dot_tn(left, right):
    return lax.dot_general(left, right, (((0,), (0,)), ((), ())), preferred_element_type=f32)


def halves(value):
    top = value.astype(bf16)
    return top, (value - top.astype(f32)).astype(bf16)


def kernel(
    x_hbm,
    frc_hbm,
    cot_hbm,
    mat_hbm,
    bias_hbm,
    lat_hbm,
    lc_hbm,
    bk_hbm,
    bi_hbm,
    ov,
    gv,
    blk,
    fin,
    xv,
    fv,
    cv,
    mat,
    wsh,
    bias,
    lat_in,
    lc,
    bk,
    bi,
    s1,
    r1,
    s2,
    r2,
    s3,
    r3,
    s4,
    r4,
    lq,
    lp,
    lqt,
    lpt,
    rows,
    cx,
    pex,
    fac,
    fil,
    kap,
    qs,
    wz,
    wrow,
    wb,
    wflat,
    we,
    ww,
    w5,
    wd,
    lch,
    ff,
    hid,
    gel,
    dwe,
    dww,
    dw5,
    dwd,
    db,
    gf,
    rk,
    rh,
    rx,
    s1r,
    ry,
    s2r,
    rw,
    wide,
    pps,
    ppr,
    px,
    pxr,
    pz,
    pzr,
    pzl,
    pzlr,
    tot,
    pgr,
    xsem,
    isem,
    ssem,
    rsem,
    gs,
    gr,
):
    xme = lax.axis_index("dp")
    me = lax.axis_index("lat")
    zme = lax.div(me, 8)
    bme = lax.rem(me, 8)
    yme = lax.div(bme, 2)
    odd = lax.rem(me, 2)

    def x_copy(ch):
        part = pl.ds(2 * ch, 2)
        return pltpu.make_async_copy(x_hbm.at[part], xv.at[part], xsem.at[ch])

    loads = [
        pltpu.make_async_copy(bk_hbm, bk, isem.at[0]),
        pltpu.make_async_copy(mat_hbm, mat, isem.at[1]),
        pltpu.make_async_copy(bias_hbm, bias, isem.at[2]),
        pltpu.make_async_copy(lc_hbm, lc, isem.at[3]),
        pltpu.make_async_copy(bi_hbm, bi, isem.at[4]),
        pltpu.make_async_copy(frc_hbm, fv, isem.at[5]),
        pltpu.make_async_copy(cot_hbm, cv, isem.at[6]),
        pltpu.make_async_copy(lat_hbm, lat_in, isem.at[9]),
    ]
    loads[0].start()
    for ch in range(CH):
        x_copy(ch).start()
    for load in loads[1:]:
        load.start()

    barrier = pltpu.get_barrier_semaphore()

    def greet(step, carry):
        pl.semaphore_signal(
            barrier, inc=1, device_id={"lat": lax.rem(me + step, LATS)}, device_id_type=MESH
        )
        return carry

    lax.fori_loop(1, LATS, greet, 0)
    for step in range(1, XS):
        pl.semaphore_signal(
            barrier, inc=1, device_id={"dp": lax.rem(xme + step, XS)}, device_id_type=MESH
        )

    sub8 = lax.broadcasted_iota(jnp.int32, (LATS // 2, 8, 128), 1)
    lower = sub8 < 4

    def lat_copy(src, dst, send, recv, peer):
        return pltpu.make_async_remote_copy(
            src_ref=src,
            dst_ref=dst,
            send_sem=send,
            recv_sem=recv,
            device_id={"lat": peer},
            device_id_type=MESH,
        )

    def dp_copy(src, dst, send, recv, peer):
        return pltpu.make_async_remote_copy(
            src_ref=src,
            dst_ref=dst,
            send_sem=send,
            recv_sem=recv,
            device_id={"dp": peer},
            device_id_type=MESH,
        )

    def drain(ref, sem):
        pltpu.make_async_copy(ref, ref, sem).wait()

    def exchange(phase, src, dst, ch):
        def one(step, carry):
            peer = lax.rem(me + 9 * step, LATS)
            lat_copy(
                src.at[ch, peer], dst.at[ch, me], ssem.at[phase, ch], rsem.at[phase, ch], peer
            ).start()
            return carry

        lax.fori_loop(1, LATS, one, 0)
        dst[ch, me] = src[ch, me]

    def arrived(phase, dst, ch):
        drain(dst.at[ch, pl.ds(0, LATS - 1)], rsem.at[phase, ch])

    def to_plane(src_of, dst, number):
        for step in range(1, 8):
            other = lax.rem(bme + step, 8)
            lat_copy(src_of(other), dst, gs.at[number], gr.at[number], zme * 8 + other).start()

    def to_column(src, dst, number):
        for step in range(1, 8):
            other = lax.rem(zme + step, 8)
            lat_copy(src, dst, gs.at[number], gr.at[number], other * 8 + bme).start()

    def to_line(src_of, dst, number):
        for step in range(1, XS):
            other = lax.rem(xme + step, XS)
            dp_copy(src_of(other), dst, gs.at[number], gr.at[number], other).start()

    def pack(first, second):
        evens = []
        odds = []
        for globe in range(2):
            lanes = slice(globe * 128, globe * 128 + 128)
            plain = first[:, lanes].reshape(LATS // 2, 8, 128)
            turned = second[:, lanes].reshape(LATS // 2, 8, 128)
            evens.append(jnp.where(lower, plain, turned))
            odds.append(jnp.where(lower, turned, plain))
        even = jnp.concatenate(evens, axis=1).astype(bf16)
        other = jnp.concatenate(odds, axis=1).astype(bf16)
        return jnp.stack([even, other], axis=1).reshape(LATS, 16, 128)

    def unpack(tiles, row):
        pairs = tiles.astype(f32).reshape(LATS // 2, 2, 16, 128)
        straight = jnp.where(row == 0, 1, 0)
        pick = jnp.where(lower, 1, 0) == straight
        sides = []
        for globe in range(2):
            even = pairs[:, 0, globe * 8 : globe * 8 + 8]
            other = pairs[:, 1, globe * 8 : globe * 8 + 8]
            sides.append(jnp.where(pick, even, other).reshape(2 * MW, 128))
        return jnp.concatenate(sides, axis=1).astype(bf16)

    loads[0].wait()

    def analyse(ch):
        x_copy(ch).wait()
        found = []
        for row in range(2):
            sides = jnp.concatenate([xv[2 * ch, row], xv[2 * ch + 1, row]], axis=1)
            found.append(dot(bk[row], sides.astype(bf16)))
        s1[ch] = pack(found[0], found[1])

    loads[1].wait()
    wsh[...] = jnp.concatenate([mat[...], jnp.zeros((6, 128), f32)], axis=0).astype(bf16)
    wz[zme] = wsh[...]

    def analyse_step(ch, carry):
        analyse(ch)

        @pl.when(ch == 0)
        def _():
            pl.semaphore_wait(barrier, LATS - 1 + XS - 1)
            to_column(wsh, wz.at[zme], 0)

        @pl.when(ch == 2)
        def _():
            drain(wz.at[pl.ds(0, 7)], gr.at[0])
            tiles = wz[...].astype(f32)
            for z in range(8):
                wrow[z * 10 : z * 10 + 10, :] = tiles[z, 0:10, :]
            wb[xme, bme] = wrow[...].astype(bf16)
            to_plane(lambda other: wb.at[xme, bme], wb.at[xme, bme], 1)

        exchange(0, s1, r1, ch)
        return carry

    lax.fori_loop(0, CH, analyse_step, 0)

    for number in (2, 3, 7):
        loads[number].wait()
    sub = lax.broadcasted_iota(jnp.int32, (128, 128), 0)
    lane = lax.broadcasted_iota(jnp.int32, (128, 128), 1)
    row_of_lane = 2 * lax.rem(lane, LATS) + lax.rem(lax.div(lane, LATS) + odd, 2)
    one_hot = jnp.where(sub == row_of_lane, 1.0, 0.0).astype(bf16)
    lat_rows = jnp.broadcast_to(lat_in[...].astype(f32), (8, 128)).astype(bf16)
    lat = dot(lat_rows, one_hot)[0:1, :]
    phi = (lat + 0.5) * (math.pi / NLAT) - 0.5 * math.pi
    mu = jnp.sin(phi)
    cos_phi = jnp.cos(phi)
    log_cos = jnp.log(cos_phi)
    m_zero = 2 * me
    k_safe = jnp.maximum(sub, 1).astype(f32)
    logs = jnp.log((2.0 * k_safe + 1.0) / (2.0 * k_safe))
    firsts = []
    for slot in range(2):
        wave = (m_zero + slot).astype(f32)
        below = (sub >= 1) & (sub <= m_zero + slot)
        total = jnp.sum(jnp.where(below, logs, 0.0), axis=0, keepdims=True)
        firsts.append(jnp.exp(-0.5 * math.log(2.0) + 0.5 * total + wave * log_cos))
        pex[slot, 0:1, :] = firsts[slot]
        degree = wave + sub.astype(f32)
        less = degree - 1.0
        square = wave * wave
        gap = jnp.where(sub == 0, 1.0, degree * degree - square)
        fac[slot, 0] = jnp.sqrt(jnp.maximum((4.0 * degree * degree - 1.0) / gap, 0.0))
        fac[slot, 1] = jnp.sqrt(
            jnp.maximum((less * less - square) / (4.0 * less * less - 1.0), 0.0)
        )
        live = degree < MW - 0.5
        ratio = degree / MW
        ratio = ratio * ratio
        ratio = ratio * ratio
        fil[slot] = jnp.where(live, jnp.exp(-(ratio * ratio)), 0.0)
        kap[slot] = degree * (degree + 1.0) / (MW * (MW - 1.0))

    def advance(n, pairs):
        following = []
        for slot in range(2):
            latest, earlier = pairs[slot]
            up = fac[slot, 0, pl.ds(n, 1), :]
            down = fac[slot, 1, pl.ds(n, 1), :]
            now = up * (mu * latest - down * earlier)
            pex[slot, pl.ds(n, 1), :] = now
            following.append((now, latest))
        return tuple(following)

    lax.fori_loop(
        1, MW, advance, tuple((firsts[slot], jnp.zeros((1, 128), f32)) for slot in range(2))
    )

    for slot in range(2):
        keep = m_zero + slot + sub < MW
        poly = jnp.where(keep, pex[slot], 0.0)
        synth = poly * jnp.where(m_zero + slot == 0, 1.0, 2.0)
        quad = poly * ((math.pi / NLAT) * cos_phi)
        anal = quad * (1.0 / NLON)
        lp[slot] = synth.astype(bf16)
        lq[slot] = anal.astype(bf16)
        lpt[slot] = synth.T.astype(bf16)
        lqt[slot] = anal.T.astype(bf16)
        if slot == 0:
            zero_wave = jnp.sum(quad, axis=1, keepdims=True)
            zero_wave = jnp.where(me == 0, zero_wave, 0.0)
            qs[...] = jnp.broadcast_to(zero_wave, (128, 128))
    lc_top, lc_low = halves(lc[...])
    lch[0] = lc_top
    lch[1] = lc_low

    drain(wb.at[0, pl.ds(0, 7)], gr.at[1])
    own_part = wb.at[xme, pl.ds(4 * odd, 4)]
    to_line(lambda other: own_part, own_part, 2)
    drain(wb.at[pl.ds(0, 3), pl.ds(0, 4)], gr.at[2])
    for step in range(1, XS):
        part = wb.at[lax.rem(xme + step, XS), pl.ds(4 * odd, 4)]
        lat_copy(part, part, gs.at[11], gr.at[11], me + 1 - 2 * odd).start()

    drain(wb.at[pl.ds(0, 3), pl.ds(0, 4)], gr.at[11])

    def spread(line, carry):
        for b in range(8):
            tile = wb[line, b].astype(f32)
            for z in range(8):
                target = wflat.at[pl.ds(pl.multiple_of(line * 640, 8), 640)]
                begin = z * 80 + b * 10
                target[begin : begin + 10, :] = tile[z * 10 : z * 10 + 10, :]
        return carry

    lax.fori_loop(0, XS, spread, 0)
    we[...] = wflat[0:128, :].astype(bf16)
    for layer in range(4):
        for side in range(2):
            begin = 128 + 512 * layer + side
            ww[layer, :, side * 128 : side * 128 + 128] = wflat[
                pl.ds(begin, 256, stride=2), :
            ].astype(bf16)
    w5[...] = wflat[2176:2432, :].astype(bf16)
    wd[...] = wflat[2432:2560, :].astype(bf16)
    loads[4].wait()
    dwe[...] = jnp.zeros_like(dwe)
    dww[...] = jnp.zeros_like(dww)
    dw5[...] = jnp.zeros_like(dw5)
    dwd[...] = jnp.zeros_like(dwd)
    db[...] = jnp.zeros_like(db)

    def couple(value, transposed):
        top, low = halves(value)
        product = dot_nt if transposed else dot
        return product(top, lch[0]) + product(top, lch[1]) + product(low, lch[0])

    def per_slot(table):
        return jnp.concatenate([table[0]] * 4 + [table[1]] * 4, axis=0)

    def gather_rows(tiles, slot):
        if slot == 0:
            rows[...] = tiles.astype(f32).reshape(1024, 128)
        sides = []
        for globe in range(2):
            for part in range(2):
                begin = globe * 8 + slot * 2 + part
                sides.append(
                    jnp.concatenate(
                        [rows[pl.ds(begin + 4 * k, LATS, stride=16), :] for k in range(2)], axis=0
                    )
                )
        return jnp.concatenate(sides, axis=1).astype(bf16)

    def to_coefficients(table, tiles):
        blocks = []
        for slot in range(2):
            found = dot(table[slot], gather_rows(tiles, slot))
            blocks += [found[:, k * 128 : k * 128 + 128] for k in range(4)]
        return blocks

    def to_tiles(table, blocks):
        for slot in range(2):
            wide_low = jnp.concatenate(blocks[4 * slot : 4 * slot + 4], axis=1).astype(bf16)
            found = dot(table[slot], wide_low)
            for globe in range(2):
                for part in range(2):
                    begin = globe * 8 + slot * 2 + part
                    lanes = slice((globe * 2 + part) * 128, (globe * 2 + part) * 128 + 128)
                    for k in range(2):
                        rows[pl.ds(begin + 4 * k, LATS, stride=16), :] = found[
                            k * LATS : k * LATS + LATS, lanes
                        ]
        return rows[...].astype(bf16).reshape(LATS, 16, 128)

    def cut(value):
        return [value[c * 128 : c * 128 + 128] for c in range(8)]

    def dynamics(ch, carry):
        arrived(0, r1, ch)
        blocks = to_coefficients(lq, r1[ch])
        coef = jnp.concatenate(blocks, axis=0)
        coef_low = coef.astype(bf16)
        cx[ch] = coef_low
        blocks = cut(coef + dot(coef_low, we[...]))
        constant = qs[...] * bias[0:1, :]
        blocks[0] = blocks[0] + constant
        blocks[2] = blocks[2] + constant
        coef = jnp.concatenate(blocks, axis=0)
        coef = per_slot(fil) * (coef - per_slot(kap) * couple(coef, False))
        s2[ch] = to_tiles(lpt, cut(coef))
        exchange(1, s2, r2, ch)
        return carry

    lax.fori_loop(0, CH, dynamics, 0)

    loads[5].wait()
    loads[6].wait()
    c_zero = math.sqrt(2.0 / math.pi)
    c_one = 0.044715

    def bias_row(index, count):
        return jnp.concatenate([bias[index + k : index + k + 1, :] for k in range(count)], axis=1)

    def add_bias(index, value):
        total = jnp.sum(value, axis=0, keepdims=True)
        for k in range(value.shape[1] // 128):
            db[index + k : index + k + 1, :] += total[:, k * 128 : k * 128 + 128]

    def two(ref, ch, row):
        return jnp.concatenate([ref[2 * ch, row], ref[2 * ch + 1, row]], axis=0)

    def columns(ch):
        def block(row, carry):
            grid = dot(bi[row], unpack(r2[ch], row))
            dynamic = jnp.concatenate([grid[:, 0:128], grid[:, 128:256]], axis=0)
            hidden = jnp.concatenate([dynamic.astype(bf16), two(fv, ch, row)], axis=1)
            hid[0] = hidden
            for layer in range(4):
                pre = dot(hidden, ww[layer]) + bias_row(1 + 2 * layer, 2)
                square = pre * pre
                inner = pre * (c_zero + (c_zero * c_one) * square)
                bent = jnp.tanh(inner)
                half = 0.5 * pre
                hidden = (half + half * bent).astype(bf16)
                slope = half * (c_zero + (3.0 * c_zero * c_one) * square)
                gel[layer] = (0.5 + 0.5 * bent) + slope * (1.0 - bent * bent)
                hid[layer + 1] = hidden
            middle = dynamic + dot(hidden, w5[...]) + bias_row(9, 1)
            middle_low = middle.astype(bf16)
            output = middle + dot(middle_low, wd[...]) + bias_row(10, 1)
            ov[2 * ch, row] = output[0:256]
            ov[2 * ch + 1, row] = output[256:512]
            upstream = two(cv, ch, row)
            up_low = upstream.astype(bf16)
            dwd[...] += dot_tn(middle_low, up_low)
            add_bias(10, upstream)
            back_mid = upstream + dot_nt(up_low, wd[...])
            mid_low = back_mid.astype(bf16)
            dw5[...] += dot_tn(hidden, mid_low)
            add_bias(9, back_mid)
            back = dot_nt(mid_low, w5[...])
            for layer in (3, 2, 1, 0):
                back_pre = gel[layer] * back
                pre_low = back_pre.astype(bf16)
                dww[layer] += dot_tn(hid[layer], pre_low)
                add_bias(1 + 2 * layer, back_pre)
                if layer > 0:
                    back = dot_nt(pre_low, ww[layer])
                else:
                    back = dot_nt(pre_low, ww[0, 0:128, :])
            back_low = (back_mid + back).astype(bf16)
            sides = jnp.concatenate([back_low[0:256], back_low[256:512]], axis=1)
            ff[row] = dot(bk[row], sides)
            return carry

        lax.fori_loop(0, 2, block, 0)
        s3[ch] = pack(ff[0], ff[1])
        exchange(2, s3, r3, ch)

    def adjoint(ch):
        arrived(2, r3, ch)
        back = jnp.concatenate(to_coefficients(lp, r3[ch]), axis=0)
        back = per_slot(fil) * back
        back = back - couple(per_slot(kap) * back, True)
        back_low = back.astype(bf16)
        dwe[...] += dot_tn(cx[ch], back_low)
        flat = qs[...] * (back[0:128] + back[256:384])
        db[0:1, :] += jnp.sum(flat, axis=0, keepdims=True)
        back = back + dot_nt(back_low, we[...])
        s4[ch] = to_tiles(lqt, cut(back))

    def grad_core():
        gf[0:128, :] = jnp.zeros((128, 128), f32)
        for layer in range(4):
            for side in range(2):
                begin = 128 + 512 * layer + side
                gf[pl.ds(begin, 256, stride=2), :] = dww[layer, :, side * 128 : side * 128 + 128]
        gf[2176:2432, :] = dw5[...]
        gf[2432:2560, :] = dwd[...]

        def one(part, carry):
            begin = pl.multiple_of(part * 160 + 80 * (1 - odd), 8)
            lat_copy(
                gf.at[pl.ds(begin, 80)], rk.at[part], gs.at[12], gr.at[12], me + 1 - 2 * odd
            ).start()
            return carry

        lax.fori_loop(0, 16, one, 0)

    def grad_line():
        drain(rk, gr.at[12])

        def one(part, carry):
            begin = pl.multiple_of(part * 160 + 80 * odd, 8)
            total = rk[part] + gf[pl.ds(begin, 80), :]
            rk[part] = total
            rh[part] = total.astype(bf16)
            return carry

        lax.fori_loop(0, 16, one, 0)
        to_line(lambda other: rh.at[pl.ds(4 * other, 4)], rx.at[xme], 3)

    def grad_row():
        drain(rx.at[pl.ds(0, 3)], gr.at[3])
        total = rk[pl.ds(4 * xme, 4)]
        for step in range(1, XS):
            total = total + rx[lax.rem(xme + step, XS)].astype(f32)
        s1r[...] = total
        for step in range(1, 4):
            other = lax.rem(yme + step, 4)
            peer = zme * 8 + other * 2 + odd
            lat_copy(s1r.at[other], ry.at[yme], gs.at[4], gr.at[4], peer).start()

    def grad_column():
        drain(ry.at[pl.ds(0, 3)], gr.at[4])
        total = s1r[yme]
        for step in range(1, 4):
            total = total + ry[lax.rem(yme + step, 4)]
        for b in range(8):
            begin = 8 * (10 * b // 8)
            s2r[b] = total[begin : begin + 16].astype(bf16)
        for step in range(8):
            other = lax.rem(bme + step, 8)
            peer = bme * 8 + other

            @pl.when(peer != me)
            def _():
                lat_copy(
                    s2r.at[other], rw.at[zme], gs.at[5], gr.at[5], peer
                ).start()

            @pl.when(peer == me)
            def _():
                rw[zme] = s2r[other]

    def turn_bytes(sem):
        @pl.when(bme == zme)
        def _():
            drain(rw.at[pl.ds(0, 7)], sem)

        @pl.when(bme != zme)
        def _():
            drain(rw, sem)

    def grad_block():
        turn_bytes(gr.at[5])
        total = rw[0].astype(f32)
        for z in range(1, 8):
            total = total + rw[z].astype(f32)
        row = lax.broadcasted_iota(jnp.int32, (16, 128), 0)
        begin = 2 * lax.rem(bme, 4)
        total = jnp.where((row >= begin) & (row < begin + 10), total, 0.0)
        blk[...] = total
        return total * total

    def forward_steps(ch, carry):
        arrived(1, r2, ch)
        columns(ch)
        return carry

    lax.fori_loop(0, CH, forward_steps, 0)
    grad_core()

    def adjoint_steps(ch, carry):
        adjoint(ch)

        @pl.when(ch == 0)
        def _():
            exchange(3, s4, r4, 0)
            grad_line()

        @pl.when(ch == 1)
        def _():
            grad_row()

        @pl.when(ch == 2)
        def _():
            grad_column()

        return carry

    lax.fori_loop(0, CH, adjoint_steps, 0)

    for b in range(8):
        pps[b, 0:16, :] = dwe[b * 16 : b * 16 + 16, :]
        pps[b, 16:32, :] = db[...]
    to_plane(lambda other: pps.at[other], ppr.at[bme], 7)
    exchange(3, s4, r4, 1)

    def last_line():
        drain(ppr.at[pl.ds(0, 7)], gr.at[7])
        total = pps[bme]
        for step in range(1, 8):
            total = total + ppr[lax.rem(bme + step, 8)]
        px[0:32, :] = total
        square = grad_block()
        px[32:40, :] = square[0:8] + square[8:16]
        to_line(lambda other: px, pxr.at[xme], 8)

    def last_column():
        drain(pxr.at[pl.ds(0, 3)], gr.at[8])
        total = px[...]
        for step in range(1, XS):
            total = total + pxr[lax.rem(xme + step, XS)]
        pzl[...] = total[0:16].astype(bf16)
        pz[...] = jnp.zeros((8, 128), f32)
        two_rows = jnp.zeros((2, 128), f32)
        for k in range(8):
            chosen = jnp.where(bme == k, 1.0, 0.0)
            two_rows = two_rows + chosen * total[16 + 2 * k : 18 + 2 * k]
        pz[0:2, :] = two_rows
        pz[2:3, :] = jnp.sum(total[32:40], axis=0, keepdims=True)
        to_column(pz, pzr.at[zme], 9)
        to_column(pzl, pzlr.at[zme], 13)

    def last_plane():
        drain(pzr.at[pl.ds(0, 7)], gr.at[9])
        drain(pzlr.at[pl.ds(0, 7)], gr.at[13])
        total = pz[...]
        wide_total = pzl[...].astype(f32)
        for step in range(1, 8):
            total = total + pzr[lax.rem(zme + step, 8)]
            wide_total = wide_total + pzlr[lax.rem(zme + step, 8)].astype(f32)
        tot[0:16, :] = wide_total
        tot[16:24, :] = total
        pgr[bme] = tot[...]
        to_plane(lambda other: tot, pgr.at[bme], 10)


    def finish(ch, carry):
        arrived(3, r4, ch)
        for row in range(2):
            grid = dot(bi[row], unpack(r4[ch], row))
            gv[2 * ch, row] = grid[:, 0:128]
            gv[2 * ch + 1, row] = grid[:, 128:256]

        @pl.when(ch == 0)
        def _():
            exchange(3, s4, r4, 2)
            last_line()
            last_column()

        @pl.when(ch == 1)
        def _():
            exchange(3, s4, r4, 3)

        @pl.when(ch == 2)
        def _():
            last_plane()

        return carry

    lax.fori_loop(0, CH, finish, 0)

    drain(pgr.at[pl.ds(0, 7)], gr.at[10])
    enc = pgr[:, 0:16, :].reshape(128, 128)
    row = lax.broadcasted_iota(jnp.int32, (128, 128), 0)
    first_row = 640 * xme + 10 * me
    wide[0:128, :] = jnp.where((row >= first_row) & (row < first_row + 10), enc, 0.0)
    wide[128:160, :] = jnp.zeros((32, 128), f32)

    @pl.when((xme == 0) & (zme < 2))
    def _():
        begin = pl.multiple_of(80 * zme + 8 * lax.div(10 * bme, 8), 8)
        blk[...] += wide[pl.ds(begin, 16), :]

    for b in range(8):
        fin[2 * b : 2 * b + 2, :] = pgr[b, 16:18, :]
    bias_total = fin[0:16, :]
    squares = (
        jnp.sum(pgr[:, 18, :]) + jnp.sum(enc * enc) + jnp.sum(bias_total * bias_total)
    )
    norm = jnp.sqrt(jnp.zeros((8, 128), f32) + squares)
    clip = jnp.minimum(1.0, clip_norm / (norm + 1e-06))
    both_clip = jnp.concatenate([clip, clip], axis=0)
    fin[0:16, :] = bias_total * both_clip
    fin[16:24, :] = norm
    blk[...] = blk[...] * both_clip

    for phase, src in enumerate((s1, s2, s3, s4)):
        for ch in range(CH):
            drain(src.at[ch, pl.ds(0, LATS - 1)], ssem.at[phase, ch])
    drain(wz.at[pl.ds(0, 7)], gs.at[0])
    drain(wb.at[0, pl.ds(0, 7)], gs.at[1])
    drain(wb.at[pl.ds(0, 3), pl.ds(0, 4)], gs.at[2])
    drain(wb.at[pl.ds(0, 3), pl.ds(0, 4)], gs.at[11])
    drain(rk, gs.at[12])
    drain(rx.at[pl.ds(0, 3)], gs.at[3])
    drain(ry.at[pl.ds(0, 3)], gs.at[4])

    turn_bytes(gs.at[5])
    drain(ppr.at[pl.ds(0, 7)], gs.at[7])
    drain(pxr.at[pl.ds(0, 3)], gs.at[8])
    drain(pzr.at[pl.ds(0, 7)], gs.at[9])
    drain(pzlr.at[pl.ds(0, 7)], gs.at[13])
    drain(pgr.at[pl.ds(0, 7)], gs.at[10])


def adam_update(weights, moment, second, grads, lost_one, lost_two):
    moment_new = beta_one * moment + (1.0 - beta_one) * grads
    second_new = beta_two * second + (1.0 - beta_two) * grads * grads
    moment_hat = moment_new / lost_one
    second_hat = second_new / lost_two
    weights_new = weights - learn_rate * (
        moment_hat / (jnp.sqrt(second_hat) + adam_eps) + decay_rate * weights
    )
    return (weights_new, moment_new, second_new)


def update_kernel(
    so_in,
    sg_in,
    blk,
    fin,
    mat,
    mat_m,
    mat_s,
    bias,
    bias_m,
    bias_s,
    steps,
    so_out,
    sg_out,
    mat_grad,
    mat_new,
    mat_copy,
    mat_m_new,
    mat_s_new,
    bias_grad,
    bias_new,
    bias_m_new,
    bias_s_new,
    norm,
    sems,
):
    def piece(number):
        which, part = number % 2, pl.ds(2 * (number // 2), 2)
        return pltpu.make_async_copy(
            (so_in, sg_in)[which].at[part], (so_out, sg_out)[which].at[part], sems.at[number]
        )

    for number in range(2 * CH):
        piece(number).start()
    count = jnp.full((1, 128), steps[0], jnp.int32).astype(f32)
    lost_one = 1.0 - jnp.exp(count * math.log(beta_one))
    lost_two = 1.0 - jnp.exp(count * math.log(beta_two))
    block = blk[...]
    place = 2 * lax.rem(lax.axis_index("lat"), 4)
    grads = jnp.zeros((10, 128), f32)
    for begin in (0, 2, 4, 6):
        grads = jnp.where(place == begin, block[begin : begin + 10], grads)
    mat_grad[...] = grads
    new, moment, second = adam_update(mat[...], mat_m[...], mat_s[...], grads, lost_one, lost_two)
    mat_new[...] = new
    mat_copy[...] = new.astype(bf16)
    mat_m_new[...] = moment
    mat_s_new[...] = second
    grads = fin[0:BIAS_ROWS, :]
    bias_grad[...] = grads
    new, moment, second = adam_update(
        bias[...], bias_m[...], bias_s[...], grads, lost_one, lost_two
    )
    bias_new[...] = new
    bias_m_new[...] = moment
    bias_s_new[...] = second
    norm[0] = jnp.max(fin[16:17, :])
    for number in range(2 * CH):
        piece(number).wait()


def local(
    state,
    forcing,
    state_cot,
    mat_master,
    mat_moment,
    mat_second,
    bias_master,
    bias_moment,
    bias_second,
    level_coupling,
    lat_of_row,
    step_count,
):
    both, turned = zonal_tables()
    any_spec = pl.BlockSpec(memory_space=pl.ANY)
    big = (8, 2, NLON, C)
    tiles = (CH, LATS, 16, 128)
    vm = pltpu.VMEM
    scratch = [
        vm(big, f32),
        vm(big, bf16),
        vm(big, f32),
        vm((10, 128), f32),
        vm((16, 128), bf16),
        vm((BIAS_ROWS, 128), f32),
        vm((1, 128), jnp.int32),
        vm((128, 128), f32),
        vm((2, 256, 256), bf16),
        vm((2, 256, 256), bf16),
        *[vm(tiles, bf16) for _ in range(8)],
        *[vm((2, 128, 128), bf16) for _ in range(4)],
        vm((1024, 128), f32),
        vm((CH, 1024, 128), bf16),
        vm((2, 128, 128), f32),
        vm((2, 2, 128, 128), f32),
        vm((2, 128, 128), f32),
        vm((2, 128, 128), f32),
        vm((128, 128), f32),
        vm((8, 16, 128), bf16),
        vm((80, 128), f32),
        vm((XS, 8, 80, 128), bf16),
        vm((2560, 128), f32),
        vm((128, 128), bf16),
        vm((4, 256, 256), bf16),
        vm((256, 128), bf16),
        vm((128, 128), bf16),
        vm((2, 128, 128), bf16),
        vm((2, 256, 256), f32),
        vm((5, 512, 256), bf16),
        vm((4, 512, 256), f32),
        vm((128, 128), f32),
        vm((4, 256, 256), f32),
        vm((256, 128), f32),
        vm((128, 128), f32),
        vm((16, 128), f32),
        vm((2560, 128), f32),
        vm((16, 80, 128), f32),
        vm((16, 80, 128), bf16),
        vm((XS, 4, 80, 128), bf16),
        vm((4, 80, 128), f32),
        vm((4, 80, 128), f32),
        vm((8, 16, 128), bf16),
        vm((8, 16, 128), bf16),
        vm((160, 128), f32),
        vm((8, 32, 128), f32),
        vm((8, 32, 128), f32),
        vm((40, 128), f32),
        vm((XS, 40, 128), f32),
        vm((8, 128), f32),
        vm((8, 8, 128), f32),
        vm((16, 128), bf16),
        vm((8, 16, 128), bf16),
        vm((24, 128), f32),
        vm((8, 24, 128), f32),
        pltpu.SemaphoreType.DMA((CH,)),
        pltpu.SemaphoreType.DMA((10,)),
        pltpu.SemaphoreType.DMA((4, CH)),
        pltpu.SemaphoreType.DMA((4, CH)),
        pltpu.SemaphoreType.DMA((14,)),
        pltpu.SemaphoreType.DMA((14,)),
    ]
    vm_spec = pl.BlockSpec(memory_space=pltpu.VMEM)
    sm_spec = pl.BlockSpec(memory_space=pltpu.SMEM)
    operands = (
        state,
        forcing,
        state_cot,
        mat_master.reshape(10, 128),
        bias_master.reshape(BIAS_ROWS, 128),
        lat_of_row.reshape(1, 128),
        level_coupling,
        jnp.asarray(both),
        jnp.asarray(turned),
    )
    held = pl.pallas_call(
        kernel,
        out_shape=(vm(big, f32), vm(big, f32), vm((16, 128), f32), vm((24, 128), f32)),
        in_specs=[any_spec] * 9,
        out_specs=(vm_spec,) * 4,
        scratch_shapes=scratch,
        compiler_params=pltpu.CompilerParams(
            collective_id=0, has_side_effects=True, vmem_limit_bytes=56 * 1024 * 1024
        ),
        cost_estimate=pl.CostEstimate(
            flops=16 * 10**9, bytes_accessed=10 * 2**20, transcendentals=4 * 10**6
        ),
        name="column_step",
    )(*[pltpu.with_memory_space_constraint(part, pltpu.HBM) for part in operands])

    mat_shape = jax.ShapeDtypeStruct((10, 128), f32)
    bias_shape = jax.ShapeDtypeStruct((BIAS_ROWS, 128), f32)
    results = pl.pallas_call(
        update_kernel,
        out_shape=(
            jax.ShapeDtypeStruct(big, f32),
            jax.ShapeDtypeStruct(big, f32),
            mat_shape,
            mat_shape,
            jax.ShapeDtypeStruct((10, 128), bf16),
            mat_shape,
            mat_shape,
            bias_shape,
            bias_shape,
            bias_shape,
            bias_shape,
            jax.ShapeDtypeStruct((1,), f32),
        ),
        in_specs=[vm_spec] * 10 + [sm_spec],
        out_specs=(any_spec,) * 2 + (vm_spec,) * 9 + (sm_spec,),
        scratch_shapes=[pltpu.SemaphoreType.DMA((2 * CH,))],
        compiler_params=pltpu.CompilerParams(vmem_limit_bytes=16 * 1024 * 1024),
        cost_estimate=pl.CostEstimate(flops=10**5, bytes_accessed=8 * 2**20, transcendentals=10**4),
        name="weight_step",
    )(
        *[pltpu.with_memory_space_constraint(part, pltpu.VMEM) for part in held],
        mat_master.reshape(10, 128),
        mat_moment.reshape(10, 128),
        mat_second.reshape(10, 128),
        bias_master.reshape(BIAS_ROWS, 128),
        bias_moment.reshape(BIAS_ROWS, 128),
        bias_second.reshape(BIAS_ROWS, 128),
        step_count,
    )
    return results[0:2] + tuple(part.reshape(-1) for part in results[2:])


def solution(mesh):
    columns = P("dp", "lat", None, None)
    flat = P(("dp", "lat"))
    return jax.shard_map(
        local,
        mesh=mesh,
        in_specs=(columns,) * 3 + (flat,) * 3 + (P(),) * 6,
        out_specs=(columns,) * 2 + (flat,) * 5 + (P(),) * 5,
        check_vma=False,
    )
```

```python
import functools
import math

import jax
import jax.numpy as jnp
import ml_dtypes
import numpy as np
from jax import lax
from jax.experimental import pallas as pl
from jax.experimental.pallas import tpu as pltpu
from jax.sharding import PartitionSpec as P

C = 128
F = 128
H = 256
NLAT = 128
NLON = 256
MW = 128
CH = 4
LATS = 64
XS = 4
BIAS_ROWS = 11

beta_one = 0.9
beta_two = 0.95
learn_rate = 0.3
decay_rate = 0.1
adam_eps = 1e-08
clip_norm = 1.0

MESH = pl.DeviceIdType.MESH
f32 = jnp.float32
bf16 = jnp.bfloat16


def zonal_tables():
    wave = np.arange(MW)
    turns = wave[:, None] * np.arange(NLON)[None, :] % NLON
    angle = turns * (2.0 * np.pi / NLON)
    rows = np.stack([np.cos(angle), -np.sin(angle)], axis=1).reshape(2 * MW, NLON)
    swapped = rows.reshape(MW // 4, 2, 4, NLON)[:, ::-1].reshape(2 * MW, NLON)
    both = np.stack([rows, swapped])
    turned = np.swapaxes(both, 1, 2)
    return both.astype(ml_dtypes.bfloat16), turned.astype(ml_dtypes.bfloat16)


def dot(left, right):
    return jnp.dot(left, right, preferred_element_type=f32)


def dot_nt(left, right):
    return lax.dot_general(left, right, (((1,), (1,)), ((), ())), preferred_element_type=f32)


def dot_tn(left, right):
    return lax.dot_general(left, right, (((0,), (0,)), ((), ())), preferred_element_type=f32)


def halves(value):
    top = value.astype(bf16)
    return top, (value - top.astype(f32)).astype(bf16)


def kernel(
    x_hbm,
    frc_hbm,
    cot_hbm,
    mat_hbm,
    bias_hbm,
    lat_hbm,
    lc_hbm,
    bk_hbm,
    bi_hbm,
    ov,
    gv,
    blk,
    fin,
    xv,
    fv,
    cv,
    mat,
    wsh,
    bias,
    lat_in,
    lc,
    bk,
    bi,
    s1,
    r1,
    s2,
    r2,
    s3,
    r3,
    s4,
    r4,
    lq,
    lp,
    lqt,
    lpt,
    rows,
    cx,
    pex,
    fac,
    fil,
    kap,
    qs,
    wz,
    wrow,
    wb,
    wflat,
    we,
    ww,
    w5,
    wd,
    lch,
    ff,
    hid,
    gel,
    dwe,
    dww,
    dw5,
    dwd,
    db,
    gf,
    rk,
    rh,
    rx,
    s1r,
    ry,
    s2r,
    rw,
    wide,
    pps,
    ppr,
    px,
    pxr,
    pz,
    pzr,
    pzl,
    pzlr,
    tot,
    pgr,
    xsem,
    isem,
    ssem,
    rsem,
    gs,
    gr,
):
    xme = lax.axis_index("dp")
    me = lax.axis_index("lat")
    zme = lax.div(me, 8)
    bme = lax.rem(me, 8)
    yme = lax.div(bme, 2)
    odd = lax.rem(me, 2)

    barrier = pltpu.get_barrier_semaphore()

    def greet(step, carry):
        pl.semaphore_signal(
            barrier, inc=1, device_id={"lat": lax.rem(me + LATS - step, LATS)}, device_id_type=MESH
        )
        return carry

    lax.fori_loop(1, LATS, greet, 0)
    for step in range(1, XS):
        pl.semaphore_signal(
            barrier, inc=1, device_id={"dp": lax.rem(xme + step, XS)}, device_id_type=MESH
        )

    def x_copy(ch):
        part = pl.ds(2 * ch, 2)
        return pltpu.make_async_copy(x_hbm.at[part], xv.at[part], xsem.at[ch])

    loads = [
        pltpu.make_async_copy(bk_hbm, bk, isem.at[0]),
        pltpu.make_async_copy(mat_hbm, mat, isem.at[1]),
        pltpu.make_async_copy(bias_hbm, bias, isem.at[2]),
        pltpu.make_async_copy(lc_hbm, lc, isem.at[3]),
        pltpu.make_async_copy(bi_hbm, bi, isem.at[4]),
        pltpu.make_async_copy(frc_hbm, fv, isem.at[5]),
        pltpu.make_async_copy(cot_hbm, cv, isem.at[6]),
        pltpu.make_async_copy(lat_hbm, lat_in, isem.at[9]),
    ]
    loads[0].start()
    for ch in range(CH):
        x_copy(ch).start()
    for load in loads[1:]:
        load.start()

    sub8 = lax.broadcasted_iota(jnp.int32, (LATS // 2, 8, 128), 1)
    lower = sub8 < 4

    def lat_copy(src, dst, send, recv, peer):
        return pltpu.make_async_remote_copy(
            src_ref=src,
            dst_ref=dst,
            send_sem=send,
            recv_sem=recv,
            device_id={"lat": peer},
            device_id_type=MESH,
        )

    def dp_copy(src, dst, send, recv, peer):
        return pltpu.make_async_remote_copy(
            src_ref=src,
            dst_ref=dst,
            send_sem=send,
            recv_sem=recv,
            device_id={"dp": peer},
            device_id_type=MESH,
        )

    def drain(ref, sem):
        pltpu.make_async_copy(ref, ref, sem).wait()

    def exchange(phase, src, dst, ch):
        def one(step, carry):
            peer = lax.rem(me + LATS - step, LATS)
            lat_copy(
                src.at[ch, peer], dst.at[ch, me], ssem.at[phase, ch], rsem.at[phase, ch], peer
            ).start()
            return carry

        lax.fori_loop(1, LATS, one, 0)
        dst[ch, me] = src[ch, me]

    def arrived(phase, dst, ch):
        drain(dst.at[ch, pl.ds(0, LATS - 1)], rsem.at[phase, ch])

    def to_plane(src_of, dst, number):
        for step in range(1, 8):
            other = lax.rem(bme + step, 8)
            lat_copy(src_of(other), dst, gs.at[number], gr.at[number], zme * 8 + other).start()

    def to_column(src, dst, number):
        for step in range(1, 8):
            other = lax.rem(zme + step, 8)
            lat_copy(src, dst, gs.at[number], gr.at[number], other * 8 + bme).start()

    def to_line(src_of, dst, number):
        for step in range(1, XS):
            other = lax.rem(xme + step, XS)
            dp_copy(src_of(other), dst, gs.at[number], gr.at[number], other).start()

    def pack(first, second):
        evens = []
        odds = []
        for globe in range(2):
            lanes = slice(globe * 128, globe * 128 + 128)
            plain = first[:, lanes].reshape(LATS // 2, 8, 128)
            turned = second[:, lanes].reshape(LATS // 2, 8, 128)
            evens.append(jnp.where(lower, plain, turned))
            odds.append(jnp.where(lower, turned, plain))
        even = jnp.concatenate(evens, axis=1).astype(bf16)
        other = jnp.concatenate(odds, axis=1).astype(bf16)
        return jnp.stack([even, other], axis=1).reshape(LATS, 16, 128)

    def unpack(tiles, row):
        pairs = tiles.astype(f32).reshape(LATS // 2, 2, 16, 128)
        straight = jnp.where(row == 0, 1, 0)
        pick = jnp.where(lower, 1, 0) == straight
        sides = []
        for globe in range(2):
            even = pairs[:, 0, globe * 8 : globe * 8 + 8]
            other = pairs[:, 1, globe * 8 : globe * 8 + 8]
            sides.append(jnp.where(pick, even, other).reshape(2 * MW, 128))
        return jnp.concatenate(sides, axis=1).astype(bf16)

    loads[0].wait()

    def analyse(ch):
        x_copy(ch).wait()
        found = []
        for row in range(2):
            sides = jnp.concatenate([xv[2 * ch, row], xv[2 * ch + 1, row]], axis=1)
            found.append(dot(bk[row], sides.astype(bf16)))
        s1[ch] = pack(found[0], found[1])

    loads[1].wait()
    wsh[...] = jnp.concatenate([mat[...], jnp.zeros((6, 128), f32)], axis=0).astype(bf16)
    wz[zme] = wsh[...]

    def analyse_step(ch, carry):
        analyse(ch)

        @pl.when(ch == 0)
        def _():
            pl.semaphore_wait(barrier, LATS - 1 + XS - 1)
            to_column(wsh, wz.at[zme], 0)

        @pl.when(ch == 2)
        def _():
            drain(wz.at[pl.ds(0, 7)], gr.at[0])
            tiles = wz[...].astype(f32)
            for z in range(8):
                wrow[z * 10 : z * 10 + 10, :] = tiles[z, 0:10, :]
            wb[xme, bme] = wrow[...].astype(bf16)
            to_plane(lambda other: wb.at[xme, bme], wb.at[xme, bme], 1)

        exchange(0, s1, r1, ch)
        return carry

    lax.fori_loop(0, CH, analyse_step, 0)

    for number in (2, 3, 7):
        loads[number].wait()
    sub = lax.broadcasted_iota(jnp.int32, (128, 128), 0)
    lane = lax.broadcasted_iota(jnp.int32, (128, 128), 1)
    row_of_lane = 2 * lax.rem(lane, LATS) + lax.rem(lax.div(lane, LATS) + odd, 2)
    one_hot = jnp.where(sub == row_of_lane, 1.0, 0.0).astype(bf16)
    lat_rows = jnp.broadcast_to(lat_in[...].astype(f32), (8, 128)).astype(bf16)
    lat = dot(lat_rows, one_hot)[0:1, :]
    phi = (lat + 0.5) * (math.pi / NLAT) - 0.5 * math.pi
    mu = jnp.sin(phi)
    cos_phi = jnp.cos(phi)
    log_cos = jnp.log(cos_phi)
    m_zero = 2 * me
    k_safe = jnp.maximum(sub, 1).astype(f32)
    logs = jnp.log((2.0 * k_safe + 1.0) / (2.0 * k_safe))
    firsts = []
    for slot in range(2):
        wave = (m_zero + slot).astype(f32)
        below = (sub >= 1) & (sub <= m_zero + slot)
        total = jnp.sum(jnp.where(below, logs, 0.0), axis=0, keepdims=True)
        firsts.append(jnp.exp(-0.5 * math.log(2.0) + 0.5 * total + wave * log_cos))
        pex[slot, 0:1, :] = firsts[slot]
        degree = wave + sub.astype(f32)
        less = degree - 1.0
        square = wave * wave
        gap = jnp.where(sub == 0, 1.0, degree * degree - square)
        fac[slot, 0] = jnp.sqrt(jnp.maximum((4.0 * degree * degree - 1.0) / gap, 0.0))
        fac[slot, 1] = jnp.sqrt(
            jnp.maximum((less * less - square) / (4.0 * less * less - 1.0), 0.0)
        )
        live = degree < MW - 0.5
        ratio = degree / MW
        ratio = ratio * ratio
        ratio = ratio * ratio
        fil[slot] = jnp.where(live, jnp.exp(-(ratio * ratio)), 0.0)
        kap[slot] = degree * (degree + 1.0) / (MW * (MW - 1.0))

    def advance(n, pairs):
        following = []
        for slot in range(2):
            latest, earlier = pairs[slot]
            up = fac[slot, 0, pl.ds(n, 1), :]
            down = fac[slot, 1, pl.ds(n, 1), :]
            now = up * (mu * latest - down * earlier)
            pex[slot, pl.ds(n, 1), :] = now
            following.append((now, latest))
        return tuple(following)

    lax.fori_loop(
        1, MW, advance, tuple((firsts[slot], jnp.zeros((1, 128), f32)) for slot in range(2))
    )

    for slot in range(2):
        keep = m_zero + slot + sub < MW
        poly = jnp.where(keep, pex[slot], 0.0)
        synth = poly * jnp.where(m_zero + slot == 0, 1.0, 2.0)
        quad = poly * ((math.pi / NLAT) * cos_phi)
        anal = quad * (1.0 / NLON)
        lp[slot] = synth.astype(bf16)
        lq[slot] = anal.astype(bf16)
        lpt[slot] = synth.T.astype(bf16)
        lqt[slot] = anal.T.astype(bf16)
        if slot == 0:
            zero_wave = jnp.sum(quad, axis=1, keepdims=True)
            zero_wave = jnp.where(me == 0, zero_wave, 0.0)
            qs[...] = jnp.broadcast_to(zero_wave, (128, 128))
    lc_top, lc_low = halves(lc[...])
    lch[0] = lc_top
    lch[1] = lc_low

    drain(wb.at[0, pl.ds(0, 7)], gr.at[1])
    own_part = wb.at[xme, pl.ds(4 * odd, 4)]
    to_line(lambda other: own_part, own_part, 2)
    drain(wb.at[pl.ds(0, 3), pl.ds(0, 4)], gr.at[2])
    for step in range(1, XS):
        part = wb.at[lax.rem(xme + step, XS), pl.ds(4 * odd, 4)]
        lat_copy(part, part, gs.at[11], gr.at[11], me + 1 - 2 * odd).start()

    drain(wb.at[pl.ds(0, 3), pl.ds(0, 4)], gr.at[11])

    def spread(line, carry):
        for b in range(8):
            tile = wb[line, b].astype(f32)
            for z in range(8):
                target = wflat.at[pl.ds(pl.multiple_of(line * 640, 8), 640)]
                begin = z * 80 + b * 10
                target[begin : begin + 10, :] = tile[z * 10 : z * 10 + 10, :]
        return carry

    lax.fori_loop(0, XS, spread, 0)
    we[...] = wflat[0:128, :].astype(bf16)
    for layer in range(4):
        for side in range(2):
            begin = 128 + 512 * layer + side
            ww[layer, :, side * 128 : side * 128 + 128] = wflat[
                pl.ds(begin, 256, stride=2), :
            ].astype(bf16)
    w5[...] = wflat[2176:2432, :].astype(bf16)
    wd[...] = wflat[2432:2560, :].astype(bf16)
    loads[4].wait()
    dwe[...] = jnp.zeros_like(dwe)
    dww[...] = jnp.zeros_like(dww)
    dw5[...] = jnp.zeros_like(dw5)
    dwd[...] = jnp.zeros_like(dwd)
    db[...] = jnp.zeros_like(db)

    def couple(value, transposed):
        top, low = halves(value)
        product = dot_nt if transposed else dot
        return product(top, lch[0]) + product(top, lch[1]) + product(low, lch[0])

    def per_slot(table):
        return jnp.concatenate([table[0]] * 4 + [table[1]] * 4, axis=0)

    def gather_rows(tiles, slot):
        if slot == 0:
            rows[0:1024, :] = tiles.astype(f32).reshape(1024, 128)
        sides = []
        for globe in range(2):
            for part in range(2):
                begin = globe * 8 + slot * 2 + part
                sides.append(
                    jnp.concatenate(
                        [rows[pl.ds(begin + 4 * k, LATS, stride=16), :] for k in range(2)], axis=0
                    )
                )
        return jnp.concatenate(sides, axis=1).astype(bf16)

    def to_coefficients(table, tiles):
        blocks = []
        for slot in range(2):
            found = dot(table[slot], gather_rows(tiles, slot))
            blocks += [found[:, k * 128 : k * 128 + 128] for k in range(4)]
        return blocks

    def to_tiles(table, blocks):
        for slot in range(2):
            wide_low = jnp.concatenate(blocks[4 * slot : 4 * slot + 4], axis=1).astype(bf16)
            found = dot(table[slot], wide_low)
            for globe in range(2):
                for part in range(2):
                    begin = globe * 8 + slot * 2 + part
                    lanes = slice((globe * 2 + part) * 128, (globe * 2 + part) * 128 + 128)
                    for k in range(2):
                        rows[pl.ds(begin + 4 * k, LATS, stride=16), :] = found[
                            k * LATS : k * LATS + LATS, lanes
                        ]
        return rows[0:1024, :].astype(bf16).reshape(LATS, 16, 128)

    def cut(value):
        return [value[c * 128 : c * 128 + 128] for c in range(8)]

    def dynamics(ch, carry):
        arrived(0, r1, ch)
        blocks = to_coefficients(lq, r1[ch])
        coef = jnp.concatenate(blocks, axis=0)
        coef_low = coef.astype(bf16)
        cx[ch] = coef_low
        blocks = cut(coef + dot(coef_low, we[...]))
        constant = qs[...] * bias[0:1, :]
        blocks[0] = blocks[0] + constant
        blocks[2] = blocks[2] + constant
        coef = jnp.concatenate(blocks, axis=0)
        coef = per_slot(fil) * (coef - per_slot(kap) * couple(coef, False))
        s2[ch] = to_tiles(lpt, cut(coef))
        exchange(1, s2, r2, ch)
        return carry

    lax.fori_loop(0, CH, dynamics, 0)

    loads[5].wait()
    loads[6].wait()
    c_zero = math.sqrt(2.0 / math.pi)
    c_one = 0.044715

    def bias_row(index, count):
        return jnp.concatenate([bias[index + k : index + k + 1, :] for k in range(count)], axis=1)

    def add_bias(index, value):
        total = jnp.sum(value, axis=0, keepdims=True)
        for k in range(value.shape[1] // 128):
            db[index + k : index + k + 1, :] += total[:, k * 128 : k * 128 + 128]

    def two(ref, ch, row):
        return jnp.concatenate([ref[2 * ch, row], ref[2 * ch + 1, row]], axis=0)

    def columns(ch):
        def block(row, carry):
            grid = dot(bi[row], unpack(r2[ch], row))
            dynamic = jnp.concatenate([grid[:, 0:128], grid[:, 128:256]], axis=0)
            hidden = jnp.concatenate([dynamic.astype(bf16), two(fv, ch, row)], axis=1)
            hid[0] = hidden
            for layer in range(4):
                pre = dot(hidden, ww[layer]) + bias_row(1 + 2 * layer, 2)
                square = pre * pre
                inner = pre * (c_zero + (c_zero * c_one) * square)
                bent = jnp.tanh(inner)
                share = 0.5 + 0.5 * bent
                active = pre * share
                hidden = active.astype(bf16)
                slope = (2.0 * c_zero) + (6.0 * c_zero * c_one) * square
                gel[layer] = share + active * (slope * (1.0 - share))
                hid[layer + 1] = hidden
            middle = dynamic + dot(hidden, w5[...]) + bias_row(9, 1)
            middle_low = middle.astype(bf16)
            output = middle + dot(middle_low, wd[...]) + bias_row(10, 1)
            ov[2 * ch, row] = output[0:256]
            ov[2 * ch + 1, row] = output[256:512]
            upstream = two(cv, ch, row)
            up_low = upstream.astype(bf16)
            dwd[...] += dot_tn(middle_low, up_low)
            add_bias(10, upstream)
            back_mid = upstream + dot_nt(up_low, wd[...])
            mid_low = back_mid.astype(bf16)
            dw5[...] += dot_tn(hidden, mid_low)
            add_bias(9, back_mid)
            back = dot_nt(mid_low, w5[...])
            for layer in (3, 2, 1, 0):
                back_pre = gel[layer] * back
                pre_low = back_pre.astype(bf16)
                dww[layer] += dot_tn(hid[layer], pre_low)
                add_bias(1 + 2 * layer, back_pre)
                if layer > 0:
                    back = dot_nt(pre_low, ww[layer])
                else:
                    back = dot_nt(pre_low, ww[0, 0:128, :])
            back_low = (back_mid + back).astype(bf16)
            sides = jnp.concatenate([back_low[0:256], back_low[256:512]], axis=1)
            ff[row] = dot(bk[row], sides)
            return carry

        lax.fori_loop(0, 2, block, 0)
        s3[ch] = pack(ff[0], ff[1])
        exchange(2, s3, r3, ch)

    def adjoint(ch):
        arrived(2, r3, ch)
        back = jnp.concatenate(to_coefficients(lp, r3[ch]), axis=0)
        back = per_slot(fil) * back
        back = back - couple(per_slot(kap) * back, True)
        back_low = back.astype(bf16)
        dwe[...] += dot_tn(cx[ch], back_low)
        flat = qs[...] * (back[0:128] + back[256:384])
        db[0:1, :] += jnp.sum(flat, axis=0, keepdims=True)
        back = back + dot_nt(back_low, we[...])
        s4[ch] = to_tiles(lqt, cut(back))

    def grad_core():
        gf[0:128, :] = jnp.zeros((128, 128), f32)
        for layer in range(4):
            for side in range(2):
                begin = 128 + 512 * layer + side
                gf[pl.ds(begin, 256, stride=2), :] = dww[layer, :, side * 128 : side * 128 + 128]
        gf[2176:2432, :] = dw5[...]
        gf[2432:2560, :] = dwd[...]

        def one(part, carry):
            begin = pl.multiple_of(part * 160 + 80 * (1 - odd), 8)
            lat_copy(
                gf.at[pl.ds(begin, 80)], rk.at[part], gs.at[12], gr.at[12], me + 1 - 2 * odd
            ).start()
            return carry

        lax.fori_loop(0, 16, one, 0)

    def grad_line():
        drain(rk, gr.at[12])

        def one(part, carry):
            begin = pl.multiple_of(part * 160 + 80 * odd, 8)
            total = rk[part] + gf[pl.ds(begin, 80), :]
            rk[part] = total
            rh[part] = total.astype(bf16)
            return carry

        lax.fori_loop(0, 16, one, 0)
        to_line(lambda other: rh.at[pl.ds(4 * other, 4)], rx.at[xme], 3)

    def grad_row():
        drain(rx.at[pl.ds(0, 3)], gr.at[3])
        total = rk[pl.ds(4 * xme, 4)]
        for step in range(1, XS):
            total = total + rx[lax.rem(xme + step, XS)].astype(f32)
        s1r[...] = total
        for step in range(1, 4):
            other = lax.rem(yme + step, 4)
            peer = zme * 8 + other * 2 + odd
            lat_copy(s1r.at[other], ry.at[yme], gs.at[4], gr.at[4], peer).start()

    def grad_column():
        drain(ry.at[pl.ds(0, 3)], gr.at[4])
        total = s1r[yme]
        for step in range(1, 4):
            total = total + ry[lax.rem(yme + step, 4)]
        for b in range(8):
            begin = 8 * (10 * b // 8)
            s2r[b] = total[begin : begin + 16].astype(bf16)
        for step in range(8):
            other = lax.rem(bme + step, 8)
            peer = bme * 8 + other

            @pl.when(peer != me)
            def _():
                lat_copy(
                    s2r.at[other], rw.at[zme], gs.at[5], gr.at[5], peer
                ).start()

            @pl.when(peer == me)
            def _():
                rw[zme] = s2r[other]

    def turn_bytes(sem):
        @pl.when(bme == zme)
        def _():
            drain(rw.at[pl.ds(0, 7)], sem)

        @pl.when(bme != zme)
        def _():
            drain(rw, sem)

    def grad_block():
        turn_bytes(gr.at[5])
        total = rw[0].astype(f32)
        for z in range(1, 8):
            total = total + rw[z].astype(f32)
        row = lax.broadcasted_iota(jnp.int32, (16, 128), 0)
        begin = 2 * lax.rem(bme, 4)
        total = jnp.where((row >= begin) & (row < begin + 10), total, 0.0)
        blk[...] = total
        return total * total

    def forward_steps(ch, carry):
        arrived(1, r2, ch)
        columns(ch)
        return carry

    lax.fori_loop(0, CH, forward_steps, 0)
    grad_core()

    def adjoint_steps(ch, carry):
        adjoint(ch)

        @pl.when(ch == 0)
        def _():
            exchange(3, s4, r4, 0)
            grad_line()

        @pl.when(ch == 1)
        def _():
            grad_row()

        @pl.when(ch == 2)
        def _():
            grad_column()

        return carry

    lax.fori_loop(0, CH, adjoint_steps, 0)

    for b in range(8):
        pps[b, 0:16, :] = dwe[b * 16 : b * 16 + 16, :]
        pps[b, 16:32, :] = db[...]
    to_plane(lambda other: pps.at[other], ppr.at[bme], 7)
    exchange(3, s4, r4, 1)

    def last_line():
        drain(ppr.at[pl.ds(0, 7)], gr.at[7])
        total = pps[bme]
        for step in range(1, 8):
            total = total + ppr[lax.rem(bme + step, 8)]
        px[0:32, :] = total
        square = grad_block()
        px[32:40, :] = square[0:8] + square[8:16]
        to_line(lambda other: px, pxr.at[xme], 8)

    def last_column():
        drain(pxr.at[pl.ds(0, 3)], gr.at[8])
        total = px[...]
        for step in range(1, XS):
            total = total + pxr[lax.rem(xme + step, XS)]
        pzl[...] = total[0:16].astype(bf16)
        pz[...] = jnp.zeros((8, 128), f32)
        two_rows = jnp.zeros((2, 128), f32)
        for k in range(8):
            chosen = jnp.where(bme == k, 1.0, 0.0)
            two_rows = two_rows + chosen * total[16 + 2 * k : 18 + 2 * k]
        pz[0:2, :] = two_rows
        pz[2:3, :] = jnp.sum(total[32:40], axis=0, keepdims=True)
        to_column(pz, pzr.at[zme], 9)
        to_column(pzl, pzlr.at[zme], 13)

    def last_plane():
        drain(pzr.at[pl.ds(0, 7)], gr.at[9])
        drain(pzlr.at[pl.ds(0, 7)], gr.at[13])
        total = pz[...]
        wide_total = pzl[...].astype(f32)
        for step in range(1, 8):
            total = total + pzr[lax.rem(zme + step, 8)]
            wide_total = wide_total + pzlr[lax.rem(zme + step, 8)].astype(f32)
        tot[0:16, :] = wide_total
        tot[16:24, :] = total
        pgr[bme] = tot[...]
        to_plane(lambda other: tot, pgr.at[bme], 10)


    def finish(ch, carry):
        arrived(3, r4, ch)
        for row in range(2):
            grid = dot(bi[row], unpack(r4[ch], row))
            gv[2 * ch, row] = grid[:, 0:128]
            gv[2 * ch + 1, row] = grid[:, 128:256]

        @pl.when(ch == 0)
        def _():
            exchange(3, s4, r4, 2)
            last_line()
            last_column()

        @pl.when(ch == 1)
        def _():
            exchange(3, s4, r4, 3)

        @pl.when(ch == 2)
        def _():
            last_plane()

        return carry

    lax.fori_loop(0, CH, finish, 0)

    drain(pgr.at[pl.ds(0, 7)], gr.at[10])
    enc = pgr[:, 0:16, :].reshape(128, 128)
    row = lax.broadcasted_iota(jnp.int32, (128, 128), 0)
    first_row = 640 * xme + 10 * me
    wide[0:128, :] = jnp.where((row >= first_row) & (row < first_row + 10), enc, 0.0)
    wide[128:160, :] = jnp.zeros((32, 128), f32)

    @pl.when((xme == 0) & (zme < 2))
    def _():
        begin = pl.multiple_of(80 * zme + 8 * lax.div(10 * bme, 8), 8)
        blk[...] += wide[pl.ds(begin, 16), :]

    for b in range(8):
        fin[2 * b : 2 * b + 2, :] = pgr[b, 16:18, :]
    bias_total = fin[0:16, :]
    squares = (
        jnp.sum(pgr[:, 18, :]) + jnp.sum(enc * enc) + jnp.sum(bias_total * bias_total)
    )
    norm = jnp.sqrt(jnp.zeros((8, 128), f32) + squares)
    clip = jnp.minimum(1.0, clip_norm / (norm + 1e-06))
    both_clip = jnp.concatenate([clip, clip], axis=0)
    fin[0:16, :] = bias_total * both_clip
    fin[16:24, :] = norm
    blk[...] = blk[...] * both_clip

    for phase, src in enumerate((s1, s2, s3, s4)):
        for ch in range(CH):
            drain(src.at[ch, pl.ds(0, LATS - 1)], ssem.at[phase, ch])
    drain(wz.at[pl.ds(0, 7)], gs.at[0])
    drain(wb.at[0, pl.ds(0, 7)], gs.at[1])
    drain(wb.at[pl.ds(0, 3), pl.ds(0, 4)], gs.at[2])
    drain(wb.at[pl.ds(0, 3), pl.ds(0, 4)], gs.at[11])
    drain(rk, gs.at[12])
    drain(rx.at[pl.ds(0, 3)], gs.at[3])
    drain(ry.at[pl.ds(0, 3)], gs.at[4])

    turn_bytes(gs.at[5])
    drain(ppr.at[pl.ds(0, 7)], gs.at[7])
    drain(pxr.at[pl.ds(0, 3)], gs.at[8])
    drain(pzr.at[pl.ds(0, 7)], gs.at[9])
    drain(pzlr.at[pl.ds(0, 7)], gs.at[13])
    drain(pgr.at[pl.ds(0, 7)], gs.at[10])


def adam_update(weights, moment, second, grads, lost_one, lost_two):
    moment_new = beta_one * moment + (1.0 - beta_one) * grads
    second_new = beta_two * second + (1.0 - beta_two) * grads * grads
    moment_hat = moment_new / lost_one
    second_hat = second_new / lost_two
    weights_new = weights - learn_rate * (
        moment_hat / (jnp.sqrt(second_hat) + adam_eps) + decay_rate * weights
    )
    return (weights_new, moment_new, second_new)


def update_kernel(
    so_in,
    sg_in,
    blk,
    fin,
    mat,
    mat_m,
    mat_s,
    bias,
    bias_m,
    bias_s,
    steps,
    so_out,
    sg_out,
    mat_grad,
    mat_new,
    mat_copy,
    mat_m_new,
    mat_s_new,
    bias_grad,
    bias_new,
    bias_m_new,
    bias_s_new,
    norm,
    mat_grad_v,
    mat_new_v,
    mat_copy_v,
    mat_m_new_v,
    mat_s_new_v,
    bias_grad_v,
    bias_new_v,
    bias_m_new_v,
    bias_s_new_v,
    norm_v,
    sems,
):
    def piece(number):
        which, part = number % 2, pl.ds(2 * (number // 2), 2)
        return pltpu.make_async_copy(
            (so_in, sg_in)[which].at[part], (so_out, sg_out)[which].at[part], sems.at[number]
        )

    for number in range(2 * CH):
        piece(number).start()
    count = jnp.broadcast_to(steps[...].astype(f32), (1, 128))
    lost_one = 1.0 - jnp.exp(count * math.log(beta_one))
    lost_two = 1.0 - jnp.exp(count * math.log(beta_two))
    block = blk[...]
    place = 2 * lax.rem(lax.axis_index("lat"), 4)
    grads = jnp.zeros((10, 128), f32)
    for begin in (0, 2, 4, 6):
        grads = jnp.where(place == begin, block[begin : begin + 10], grads)
    mat_grad_v[...] = grads
    new, moment, second = adam_update(mat[...], mat_m[...], mat_s[...], grads, lost_one, lost_two)
    mat_new_v[...] = new
    mat_copy_v[...] = new.astype(bf16)
    mat_m_new_v[...] = moment
    mat_s_new_v[...] = second
    grads = fin[0:BIAS_ROWS, :]
    bias_grad_v[...] = grads
    new, moment, second = adam_update(
        bias[...], bias_m[...], bias_s[...], grads, lost_one, lost_two
    )
    bias_new_v[...] = new
    bias_m_new_v[...] = moment
    bias_s_new_v[...] = second
    norm_v[...] = fin[16:17, 0:1]
    small = [
        pltpu.make_async_copy(mat_grad_v, mat_grad, sems.at[8]),
        pltpu.make_async_copy(mat_new_v, mat_new, sems.at[9]),
        pltpu.make_async_copy(mat_copy_v, mat_copy, sems.at[10]),
        pltpu.make_async_copy(mat_m_new_v, mat_m_new, sems.at[11]),
        pltpu.make_async_copy(mat_s_new_v, mat_s_new, sems.at[12]),
        pltpu.make_async_copy(bias_grad_v, bias_grad, sems.at[13]),
        pltpu.make_async_copy(bias_new_v, bias_new, sems.at[14]),
        pltpu.make_async_copy(bias_m_new_v, bias_m_new, sems.at[15]),
        pltpu.make_async_copy(bias_s_new_v, bias_s_new, sems.at[16]),
        pltpu.make_async_copy(norm_v, norm, sems.at[17]),
    ]
    for copy in small:
        copy.start()
    for number in range(2 * CH):
        piece(number).wait()
    for copy in small:
        copy.wait()


def local(
    state,
    forcing,
    state_cot,
    mat_master,
    mat_moment,
    mat_second,
    bias_master,
    bias_moment,
    bias_second,
    level_coupling,
    lat_of_row,
    step_count,
):
    both, turned = zonal_tables()
    any_spec = pl.BlockSpec(memory_space=pl.ANY)
    big = (8, 2, NLON, C)
    tiles = (CH, LATS, 16, 128)
    vm = pltpu.VMEM
    scratch = [
        vm(big, f32),
        vm(big, bf16),
        vm(big, f32),
        vm((10, 128), f32),
        vm((16, 128), bf16),
        vm((BIAS_ROWS, 128), f32),
        vm((1, 128), jnp.int32),
        vm((128, 128), f32),
        vm((2, 256, 256), bf16),
        vm((2, 256, 256), bf16),
        *[vm(tiles, bf16) for _ in range(8)],
        *[vm((2, 128, 128), bf16) for _ in range(4)],
        vm((1040, 128), f32),
        vm((CH, 1024, 128), bf16),
        vm((2, 128, 128), f32),
        vm((2, 2, 128, 128), f32),
        vm((2, 128, 128), f32),
        vm((2, 128, 128), f32),
        vm((128, 128), f32),
        vm((8, 16, 128), bf16),
        vm((80, 128), f32),
        vm((XS, 8, 80, 128), bf16),
        vm((2560, 128), f32),
        vm((128, 128), bf16),
        vm((4, 256, 256), bf16),
        vm((256, 128), bf16),
        vm((128, 128), bf16),
        vm((2, 128, 128), bf16),
        vm((2, 256, 256), f32),
        vm((5, 512, 256), bf16),
        vm((4, 512, 256), f32),
        vm((128, 128), f32),
        vm((4, 256, 256), f32),
        vm((256, 128), f32),
        vm((128, 128), f32),
        vm((16, 128), f32),
        vm((2560, 128), f32),
        vm((16, 80, 128), f32),
        vm((16, 80, 128), bf16),
        vm((XS, 4, 80, 128), bf16),
        vm((4, 80, 128), f32),
        vm((4, 80, 128), f32),
        vm((8, 16, 128), bf16),
        vm((8, 16, 128), bf16),
        vm((160, 128), f32),
        vm((8, 32, 128), f32),
        vm((8, 32, 128), f32),
        vm((40, 128), f32),
        vm((XS, 40, 128), f32),
        vm((8, 128), f32),
        vm((8, 8, 128), f32),
        vm((16, 128), bf16),
        vm((8, 16, 128), bf16),
        vm((24, 128), f32),
        vm((8, 24, 128), f32),
        pltpu.SemaphoreType.DMA((CH,)),
        pltpu.SemaphoreType.DMA((10,)),
        pltpu.SemaphoreType.DMA((4, CH)),
        pltpu.SemaphoreType.DMA((4, CH)),
        pltpu.SemaphoreType.DMA((14,)),
        pltpu.SemaphoreType.DMA((14,)),
    ]
    vm_spec = pl.BlockSpec(memory_space=pltpu.VMEM)
    operands = (
        state,
        forcing,
        state_cot,
        mat_master.reshape(10, 128),
        bias_master.reshape(BIAS_ROWS, 128),
        lat_of_row.reshape(1, 128),
        level_coupling,
        jnp.asarray(both),
        jnp.asarray(turned),
    )
    held = pl.pallas_call(
        kernel,
        out_shape=(vm(big, f32), vm(big, f32), vm((16, 128), f32), vm((24, 128), f32)),
        in_specs=[any_spec] * 9,
        out_specs=(vm_spec,) * 4,
        scratch_shapes=scratch,
        compiler_params=pltpu.CompilerParams(
            collective_id=0, has_side_effects=True, vmem_limit_bytes=56 * 1024 * 1024
        ),
        cost_estimate=pl.CostEstimate(
            flops=16 * 10**9, bytes_accessed=10 * 2**20, transcendentals=4 * 10**6
        ),
        name="column_step",
    )(*[pltpu.with_memory_space_constraint(part, pltpu.HBM) for part in operands])

    mat_shape = jax.ShapeDtypeStruct((10, 128), f32)
    bias_shape = jax.ShapeDtypeStruct((BIAS_ROWS, 128), f32)
    results = pl.pallas_call(
        update_kernel,
        out_shape=(
            jax.ShapeDtypeStruct(big, f32),
            jax.ShapeDtypeStruct(big, f32),
            mat_shape,
            mat_shape,
            jax.ShapeDtypeStruct((10, 128), bf16),
            mat_shape,
            mat_shape,
            bias_shape,
            bias_shape,
            bias_shape,
            bias_shape,
            jax.ShapeDtypeStruct((1, 1), f32),
        ),
        in_specs=[vm_spec] * 11,
        out_specs=(any_spec,) * 12,
        scratch_shapes=[
            *[vm((10, 128), f32), vm((10, 128), f32), vm((10, 128), bf16)],
            *[vm((10, 128), f32) for _ in range(2)],
            *[vm((BIAS_ROWS, 128), f32) for _ in range(4)],
            vm((1, 1), f32),
            pltpu.SemaphoreType.DMA((2 * CH + 10,)),
        ],
        compiler_params=pltpu.CompilerParams(vmem_limit_bytes=16 * 1024 * 1024),
        cost_estimate=pl.CostEstimate(flops=10**5, bytes_accessed=8 * 2**20, transcendentals=10**4),
        name="weight_step",
    )(
        *[pltpu.with_memory_space_constraint(part, pltpu.VMEM) for part in held],
        mat_master.reshape(10, 128),
        mat_moment.reshape(10, 128),
        mat_second.reshape(10, 128),
        bias_master.reshape(BIAS_ROWS, 128),
        bias_moment.reshape(BIAS_ROWS, 128),
        bias_second.reshape(BIAS_ROWS, 128),
        step_count.reshape(1, 1),
    )
    return results[0:2] + tuple(part.reshape(-1) for part in results[2:])


def solution(mesh):
    columns = P("dp", "lat", None, None)
    flat = P(("dp", "lat"))
    return jax.shard_map(
        local,
        mesh=mesh,
        in_specs=(columns,) * 3 + (flat,) * 3 + (P(),) * 6,
        out_specs=(columns,) * 2 + (flat,) * 5 + (P(),) * 5,
        check_vma=False,
    )
```

```python
import functools
import math

import jax
import jax.numpy as jnp
import ml_dtypes
import numpy as np
from jax import lax
from jax.experimental import pallas as pl
from jax.experimental.pallas import tpu as pltpu
from jax.sharding import PartitionSpec as P

C = 128
F = 128
H = 256
NLAT = 128
NLON = 256
MW = 128
CH = 4
LATS = 64
XS = 4
BIAS_ROWS = 11

beta_one = 0.9
beta_two = 0.95
learn_rate = 0.3
decay_rate = 0.1
adam_eps = 1e-08
clip_norm = 1.0

MESH = pl.DeviceIdType.MESH
f32 = jnp.float32
bf16 = jnp.bfloat16


def zonal_tables():
    wave = np.arange(MW)
    turns = wave[:, None] * np.arange(NLON)[None, :] % NLON
    angle = turns * (2.0 * np.pi / NLON)
    rows = np.stack([np.cos(angle), -np.sin(angle)], axis=1).reshape(2 * MW, NLON)
    swapped = rows.reshape(MW // 4, 2, 4, NLON)[:, ::-1].reshape(2 * MW, NLON)
    both = np.stack([rows, swapped])
    turned = np.swapaxes(both, 1, 2)
    return both.astype(ml_dtypes.bfloat16), turned.astype(ml_dtypes.bfloat16)


def dot(left, right):
    return jnp.dot(left, right, preferred_element_type=f32)


def dot_nt(left, right):
    return lax.dot_general(left, right, (((1,), (1,)), ((), ())), preferred_element_type=f32)


def dot_tn(left, right):
    return lax.dot_general(left, right, (((0,), (0,)), ((), ())), preferred_element_type=f32)


def halves(value):
    top = value.astype(bf16)
    return top, (value - top.astype(f32)).astype(bf16)


def kernel(
    x_hbm,
    frc_hbm,
    cot_hbm,
    mat_hbm,
    bias_hbm,
    lat_hbm,
    lc_hbm,
    bk_hbm,
    bi_hbm,
    ov,
    gv,
    blk,
    fin,
    xv,
    fv,
    cv,
    mat,
    wsh,
    bias,
    lat_in,
    lc,
    bk,
    bi,
    s1,
    r1,
    s2,
    r2,
    s3,
    r3,
    s4,
    r4,
    lq,
    lp,
    lqt,
    lpt,
    rows,
    cx,
    pex,
    fac,
    fil,
    kap,
    qs,
    wz,
    wrow,
    wb,
    wflat,
    we,
    ww,
    w5,
    wd,
    lch,
    ff,
    hid,
    gel,
    dwe,
    dww,
    dw5,
    dwd,
    db,
    gf,
    rk,
    rh,
    rx,
    s1r,
    ry,
    s2r,
    rw,
    wide,
    pps,
    ppr,
    px,
    pxr,
    pz,
    pzr,
    pzl,
    pzlr,
    tot,
    pgr,
    xsem,
    isem,
    ssem,
    rsem,
    gs,
    gr,
):
    xme = lax.axis_index("dp")
    me = lax.axis_index("lat")
    zme = lax.div(me, 8)
    bme = lax.rem(me, 8)
    yme = lax.div(bme, 2)
    odd = lax.rem(me, 2)
    parity = lax.rem(odd + zme, 2)
    turn = lax.div(odd + zme, 2)

    barrier = pltpu.get_barrier_semaphore()

    def greet(step, carry):
        pl.semaphore_signal(
            barrier, inc=1, device_id={"lat": lax.rem(me + LATS - step, LATS)}, device_id_type=MESH
        )
        return carry

    lax.fori_loop(1, LATS, greet, 0)
    for step in range(1, XS):
        pl.semaphore_signal(
            barrier, inc=1, device_id={"dp": lax.rem(xme + step, XS)}, device_id_type=MESH
        )

    def x_copy(ch):
        part = pl.ds(2 * ch, 2)
        return pltpu.make_async_copy(x_hbm.at[part], xv.at[part], xsem.at[ch])

    loads = [
        pltpu.make_async_copy(bk_hbm, bk, isem.at[0]),
        pltpu.make_async_copy(mat_hbm, mat, isem.at[1]),
        pltpu.make_async_copy(bias_hbm, bias, isem.at[2]),
        pltpu.make_async_copy(lc_hbm, lc, isem.at[3]),
        pltpu.make_async_copy(bi_hbm, bi, isem.at[4]),
        pltpu.make_async_copy(frc_hbm, fv, isem.at[5]),
        pltpu.make_async_copy(cot_hbm, cv, isem.at[6]),
        pltpu.make_async_copy(lat_hbm, lat_in, isem.at[9]),
    ]
    loads[0].start()
    for ch in range(CH):
        x_copy(ch).start()
    for load in loads[1:]:
        load.start()

    sub8 = lax.broadcasted_iota(jnp.int32, (LATS // 2, 8, 128), 1)
    lower = sub8 < 4

    def lat_copy(src, dst, send, recv, peer):
        return pltpu.make_async_remote_copy(
            src_ref=src,
            dst_ref=dst,
            send_sem=send,
            recv_sem=recv,
            device_id={"lat": peer},
            device_id_type=MESH,
        )

    def dp_copy(src, dst, send, recv, peer):
        return pltpu.make_async_remote_copy(
            src_ref=src,
            dst_ref=dst,
            send_sem=send,
            recv_sem=recv,
            device_id={"dp": peer},
            device_id_type=MESH,
        )

    def drain(ref, sem):
        pltpu.make_async_copy(ref, ref, sem).wait()

    def exchange(phase, src, dst, ch):
        def one(step, carry):
            peer = lax.rem(me + LATS - step, LATS)
            lat_copy(
                src.at[ch, peer], dst.at[ch, me], ssem.at[phase, ch], rsem.at[phase, ch], peer
            ).start()
            return carry

        lax.fori_loop(1, LATS, one, 0)
        dst[ch, me] = src[ch, me]

    def arrived(phase, dst, ch):
        drain(dst.at[ch, pl.ds(0, LATS - 1)], rsem.at[phase, ch])

    def to_plane(src_of, dst, number):
        for step in range(1, 8):
            other = lax.rem(bme + step, 8)
            lat_copy(src_of(other), dst, gs.at[number], gr.at[number], zme * 8 + other).start()

    def to_column(src, dst, number):
        for step in range(1, 8):
            other = lax.rem(zme + step, 8)
            lat_copy(src, dst, gs.at[number], gr.at[number], other * 8 + bme).start()

    def to_line(src_of, dst, number):
        for step in range(1, XS):
            other = lax.rem(xme + step, XS)
            dp_copy(src_of(other), dst, gs.at[number], gr.at[number], other).start()

    def pack(first, second):
        evens = []
        odds = []
        for globe in range(2):
            lanes = slice(globe * 128, globe * 128 + 128)
            plain = first[:, lanes].reshape(LATS // 2, 8, 128)
            turned = second[:, lanes].reshape(LATS // 2, 8, 128)
            evens.append(jnp.where(lower, plain, turned))
            odds.append(jnp.where(lower, turned, plain))
        even = jnp.concatenate(evens, axis=1).astype(bf16)
        other = jnp.concatenate(odds, axis=1).astype(bf16)
        return jnp.stack([even, other], axis=1).reshape(LATS, 16, 128)

    def unpack(tiles, row):
        pairs = tiles.astype(f32).reshape(LATS // 2, 2, 16, 128)
        straight = jnp.where(row == 0, 1, 0)
        pick = jnp.where(lower, 1, 0) == straight
        sides = []
        for globe in range(2):
            even = pairs[:, 0, globe * 8 : globe * 8 + 8]
            other = pairs[:, 1, globe * 8 : globe * 8 + 8]
            sides.append(jnp.where(pick, even, other).reshape(2 * MW, 128))
        return jnp.concatenate(sides, axis=1).astype(bf16)

    loads[0].wait()

    def analyse(ch):
        x_copy(ch).wait()
        found = []
        for row in range(2):
            sides = jnp.concatenate([xv[2 * ch, row], xv[2 * ch + 1, row]], axis=1)
            found.append(dot(bk[row], sides.astype(bf16)))
        s1[ch] = pack(found[0], found[1])

    loads[1].wait()
    wsh[...] = jnp.concatenate([mat[...], jnp.zeros((6, 128), f32)], axis=0).astype(bf16)
    wz[zme] = wsh[...]

    def analyse_step(ch, carry):
        analyse(ch)

        @pl.when(ch == 0)
        def _():
            pl.semaphore_wait(barrier, LATS - 1 + XS - 1)
            to_column(wsh, wz.at[zme], 0)

        @pl.when(ch == 2)
        def _():
            drain(wz.at[pl.ds(0, 7)], gr.at[0])
            tiles = wz[...].astype(f32)
            for z in range(8):
                wrow[z * 10 : z * 10 + 10, :] = tiles[z, 0:10, :]
            wb[xme, bme] = wrow[...].astype(bf16)
            to_plane(lambda other: wb.at[xme, bme], wb.at[xme, bme], 1)

        exchange(0, s1, r1, ch)
        return carry

    lax.fori_loop(0, CH, analyse_step, 0)

    for number in (2, 3, 7):
        loads[number].wait()
    sub = lax.broadcasted_iota(jnp.int32, (128, 128), 0)
    lane = lax.broadcasted_iota(jnp.int32, (128, 128), 1)
    row_of_lane = 2 * lax.rem(lane, LATS) + lax.rem(lax.div(lane, LATS) + odd, 2)
    one_hot = jnp.where(sub == row_of_lane, 1.0, 0.0).astype(bf16)
    lat_rows = jnp.broadcast_to(lat_in[...].astype(f32), (8, 128)).astype(bf16)
    lat = dot(lat_rows, one_hot)[0:1, :]
    phi = (lat + 0.5) * (math.pi / NLAT) - 0.5 * math.pi
    mu = jnp.sin(phi)
    cos_phi = jnp.cos(phi)
    log_cos = jnp.log(cos_phi)
    m_zero = 2 * me
    k_safe = jnp.maximum(sub, 1).astype(f32)
    logs = jnp.log((2.0 * k_safe + 1.0) / (2.0 * k_safe))
    firsts = []
    for slot in range(2):
        wave = (m_zero + slot).astype(f32)
        below = (sub >= 1) & (sub <= m_zero + slot)
        total = jnp.sum(jnp.where(below, logs, 0.0), axis=0, keepdims=True)
        firsts.append(jnp.exp(-0.5 * math.log(2.0) + 0.5 * total + wave * log_cos))
        pex[slot, 0:1, :] = firsts[slot]
        degree = wave + sub.astype(f32)
        less = degree - 1.0
        square = wave * wave
        gap = jnp.where(sub == 0, 1.0, degree * degree - square)
        fac[slot, 0] = jnp.sqrt(jnp.maximum((4.0 * degree * degree - 1.0) / gap, 0.0))
        fac[slot, 1] = jnp.sqrt(
            jnp.maximum((less * less - square) / (4.0 * less * less - 1.0), 0.0)
        )
        live = degree < MW - 0.5
        ratio = degree / MW
        ratio = ratio * ratio
        ratio = ratio * ratio
        fil[slot] = jnp.where(live, jnp.exp(-(ratio * ratio)), 0.0)
        kap[slot] = degree * (degree + 1.0) / (MW * (MW - 1.0))

    def advance(n, pairs):
        following = []
        for slot in range(2):
            latest, earlier = pairs[slot]
            up = fac[slot, 0, pl.ds(n, 1), :]
            down = fac[slot, 1, pl.ds(n, 1), :]
            now = up * (mu * latest - down * earlier)
            pex[slot, pl.ds(n, 1), :] = now
            following.append((now, latest))
        return tuple(following)

    lax.fori_loop(
        1, MW, advance, tuple((firsts[slot], jnp.zeros((1, 128), f32)) for slot in range(2))
    )

    for slot in range(2):
        keep = m_zero + slot + sub < MW
        poly = jnp.where(keep, pex[slot], 0.0)
        synth = poly * jnp.where(m_zero + slot == 0, 1.0, 2.0)
        quad = poly * ((math.pi / NLAT) * cos_phi)
        anal = quad * (1.0 / NLON)
        lp[slot] = synth.astype(bf16)
        lq[slot] = anal.astype(bf16)
        lpt[slot] = synth.T.astype(bf16)
        lqt[slot] = anal.T.astype(bf16)
        if slot == 0:
            zero_wave = jnp.sum(quad, axis=1, keepdims=True)
            zero_wave = jnp.where(me == 0, zero_wave, 0.0)
            qs[...] = jnp.broadcast_to(zero_wave, (128, 128))
    lc_top, lc_low = halves(lc[...])
    lch[0] = lc_top
    lch[1] = lc_low

    drain(wb.at[0, pl.ds(0, 7)], gr.at[1])
    own_part = wb.at[xme, pl.ds(4 * odd, 4)]
    to_line(lambda other: own_part, own_part, 2)
    drain(wb.at[pl.ds(0, 3), pl.ds(0, 4)], gr.at[2])
    for step in range(1, XS):
        part = wb.at[lax.rem(xme + step, XS), pl.ds(4 * odd, 4)]
        lat_copy(part, part, gs.at[11], gr.at[11], me + 1 - 2 * odd).start()

    drain(wb.at[pl.ds(0, 3), pl.ds(0, 4)], gr.at[11])

    def spread(line, carry):
        for b in range(8):
            tile = wb[line, b].astype(f32)
            for z in range(8):
                target = wflat.at[pl.ds(pl.multiple_of(line * 640, 8), 640)]
                begin = z * 80 + b * 10
                target[begin : begin + 10, :] = tile[z * 10 : z * 10 + 10, :]
        return carry

    lax.fori_loop(0, XS, spread, 0)
    we[...] = wflat[0:128, :].astype(bf16)
    for layer in range(4):
        for side in range(2):
            begin = 128 + 512 * layer + side
            ww[layer, :, side * 128 : side * 128 + 128] = wflat[
                pl.ds(begin, 256, stride=2), :
            ].astype(bf16)
    w5[...] = wflat[2176:2432, :].astype(bf16)
    wd[...] = wflat[2432:2560, :].astype(bf16)
    loads[4].wait()
    dwe[...] = jnp.zeros_like(dwe)
    dww[...] = jnp.zeros_like(dww)
    dw5[...] = jnp.zeros_like(dw5)
    dwd[...] = jnp.zeros_like(dwd)
    db[...] = jnp.zeros_like(db)

    def couple(value, transposed):
        top, low = halves(value)
        product = dot_nt if transposed else dot
        return product(top, lch[0]) + product(top, lch[1]) + product(low, lch[0])

    def per_slot(table):
        return jnp.concatenate([table[0]] * 4 + [table[1]] * 4, axis=0)

    def gather_rows(tiles, slot):
        if slot == 0:
            rows[0:1024, :] = tiles.astype(f32).reshape(1024, 128)
        sides = []
        for globe in range(2):
            for part in range(2):
                begin = globe * 8 + slot * 2 + part
                sides.append(
                    jnp.concatenate(
                        [rows[pl.ds(begin + 4 * k, LATS, stride=16), :] for k in range(2)], axis=0
                    )
                )
        return jnp.concatenate(sides, axis=1).astype(bf16)

    def to_coefficients(table, tiles):
        blocks = []
        for slot in range(2):
            found = dot(table[slot], gather_rows(tiles, slot))
            blocks += [found[:, k * 128 : k * 128 + 128] for k in range(4)]
        return blocks

    def to_tiles(table, blocks):
        for slot in range(2):
            wide_low = jnp.concatenate(blocks[4 * slot : 4 * slot + 4], axis=1).astype(bf16)
            found = dot(table[slot], wide_low)
            for globe in range(2):
                for part in range(2):
                    begin = globe * 8 + slot * 2 + part
                    lanes = slice((globe * 2 + part) * 128, (globe * 2 + part) * 128 + 128)
                    for k in range(2):
                        rows[pl.ds(begin + 4 * k, LATS, stride=16), :] = found[
                            k * LATS : k * LATS + LATS, lanes
                        ]
        return rows[0:1024, :].astype(bf16).reshape(LATS, 16, 128)

    def cut(value):
        return [value[c * 128 : c * 128 + 128] for c in range(8)]

    def dynamics(ch, carry):
        arrived(0, r1, ch)
        blocks = to_coefficients(lq, r1[ch])
        coef = jnp.concatenate(blocks, axis=0)
        coef_low = coef.astype(bf16)
        cx[ch] = coef_low
        blocks = cut(coef + dot(coef_low, we[...]))
        constant = qs[...] * bias[0:1, :]
        blocks[0] = blocks[0] + constant
        blocks[2] = blocks[2] + constant
        coef = jnp.concatenate(blocks, axis=0)
        coef = per_slot(fil) * (coef - per_slot(kap) * couple(coef, False))
        s2[ch] = to_tiles(lpt, cut(coef))
        exchange(1, s2, r2, ch)
        return carry

    lax.fori_loop(0, CH, dynamics, 0)

    loads[5].wait()
    loads[6].wait()
    c_zero = math.sqrt(2.0 / math.pi)
    c_one = 0.044715

    def bias_row(index, count):
        return jnp.concatenate([bias[index + k : index + k + 1, :] for k in range(count)], axis=1)

    def add_bias(index, value):
        total = jnp.sum(value, axis=0, keepdims=True)
        for k in range(value.shape[1] // 128):
            db[index + k : index + k + 1, :] += total[:, k * 128 : k * 128 + 128]

    def two(ref, ch, row):
        return jnp.concatenate([ref[2 * ch, row], ref[2 * ch + 1, row]], axis=0)

    def columns(ch):
        def block(row, carry):
            grid = dot(bi[row], unpack(r2[ch], row))
            dynamic = jnp.concatenate([grid[:, 0:128], grid[:, 128:256]], axis=0)
            hidden = jnp.concatenate([dynamic.astype(bf16), two(fv, ch, row)], axis=1)
            hid[0] = hidden
            for layer in range(4):
                pre = dot(hidden, ww[layer]) + bias_row(1 + 2 * layer, 2)
                square = pre * pre
                inner = pre * (c_zero + (c_zero * c_one) * square)
                bent = jnp.tanh(inner)
                share = 0.5 + 0.5 * bent
                active = pre * share
                hidden = active.astype(bf16)
                slope = (2.0 * c_zero) + (6.0 * c_zero * c_one) * square
                gel[layer] = share + active * (slope * (1.0 - share))
                hid[layer + 1] = hidden
            middle = dynamic + dot(hidden, w5[...]) + bias_row(9, 1)
            middle_low = middle.astype(bf16)
            output = middle + dot(middle_low, wd[...]) + bias_row(10, 1)
            ov[2 * ch, row] = output[0:256]
            ov[2 * ch + 1, row] = output[256:512]
            upstream = two(cv, ch, row)
            up_low = upstream.astype(bf16)
            dwd[...] += dot_tn(middle_low, up_low)
            add_bias(10, upstream)
            back_mid = upstream + dot_nt(up_low, wd[...])
            mid_low = back_mid.astype(bf16)
            dw5[...] += dot_tn(hidden, mid_low)
            add_bias(9, back_mid)
            back = dot_nt(mid_low, w5[...])
            for layer in (3, 2, 1, 0):
                back_pre = gel[layer] * back
                pre_low = back_pre.astype(bf16)
                dww[layer] += dot_tn(hid[layer], pre_low)
                add_bias(1 + 2 * layer, back_pre)
                if layer > 0:
                    back = dot_nt(pre_low, ww[layer])
                else:
                    back = dot_nt(pre_low, ww[0, 0:128, :])
            back_low = (back_mid + back).astype(bf16)
            sides = jnp.concatenate([back_low[0:256], back_low[256:512]], axis=1)
            ff[row] = dot(bk[row], sides)
            return carry

        lax.fori_loop(0, 2, block, 0)
        s3[ch] = pack(ff[0], ff[1])
        exchange(2, s3, r3, ch)

    def adjoint(ch):
        arrived(2, r3, ch)
        back = jnp.concatenate(to_coefficients(lp, r3[ch]), axis=0)
        back = per_slot(fil) * back
        back = back - couple(per_slot(kap) * back, True)
        back_low = back.astype(bf16)
        dwe[...] += dot_tn(cx[ch], back_low)
        flat = qs[...] * (back[0:128] + back[256:384])
        db[0:1, :] += jnp.sum(flat, axis=0, keepdims=True)
        back = back + dot_nt(back_low, we[...])
        s4[ch] = to_tiles(lqt, cut(back))

    def grad_core():
        gf[0:128, :] = jnp.zeros((128, 128), f32)
        for layer in range(4):
            for side in range(2):
                begin = 128 + 512 * layer + side
                gf[pl.ds(begin, 256, stride=2), :] = dww[layer, :, side * 128 : side * 128 + 128]
        gf[2176:2432, :] = dw5[...]
        gf[2432:2560, :] = dwd[...]

        def one(part, carry):
            begin = pl.multiple_of(part * 160 + 80 * (1 - parity), 8)
            lat_copy(
                gf.at[pl.ds(begin, 80)], rk.at[part], gs.at[12], gr.at[12], me + 1 - 2 * odd
            ).start()
            return carry

        lax.fori_loop(0, 16, one, 0)

    def grad_line():
        drain(rk, gr.at[12])

        def one(part, carry):
            begin = pl.multiple_of(part * 160 + 80 * parity, 8)
            total = rk[part] + gf[pl.ds(begin, 80), :]
            rk[part] = total
            rh[part] = total.astype(bf16)
            return carry

        lax.fori_loop(0, 16, one, 0)
        to_line(lambda other: rh.at[pl.ds(4 * other, 4)], rx.at[xme], 3)

    def grad_row():
        drain(rx.at[pl.ds(0, 3)], gr.at[3])
        total = rk[pl.ds(4 * xme, 4)]
        for step in range(1, XS):
            total = total + rx[lax.rem(xme + step, XS)].astype(f32)
        s1r[...] = total
        for step in range(1, 4):
            other = lax.rem(yme + step, 4)
            peer = zme * 8 + other * 2 + odd
            lat_copy(
                s1r.at[lax.rem(other + turn, 4)], ry.at[yme], gs.at[4], gr.at[4], peer
            ).start()

    def grad_column():
        drain(ry.at[pl.ds(0, 3)], gr.at[4])
        total = s1r[lax.rem(yme + turn, 4)]
        for step in range(1, 4):
            total = total + ry[lax.rem(yme + step, 4)]
        for b in range(8):
            begin = 8 * (10 * b // 8)
            s2r[b] = total[begin : begin + 16].astype(bf16)
        for step in range(8):
            other = lax.rem(bme + step, 8)
            peer = lax.rem(bme + zme, 8) * 8 + other

            @pl.when(peer != me)
            def _():
                lat_copy(
                    s2r.at[other], rw.at[zme], gs.at[5], gr.at[5], peer
                ).start()

            @pl.when(peer == me)
            def _():
                rw[zme] = s2r[other]

    def turn_bytes(sem):
        @pl.when(bme == 0)
        def _():
            drain(rw.at[pl.ds(0, 7)], sem)

        @pl.when(bme != 0)
        def _():
            drain(rw, sem)

    def grad_block():
        turn_bytes(gr.at[5])
        total = rw[0].astype(f32)
        for z in range(1, 8):
            total = total + rw[z].astype(f32)
        row = lax.broadcasted_iota(jnp.int32, (16, 128), 0)
        begin = 2 * lax.rem(bme, 4)
        total = jnp.where((row >= begin) & (row < begin + 10), total, 0.0)
        blk[...] = total
        return total * total

    def forward_steps(ch, carry):
        arrived(1, r2, ch)
        columns(ch)
        return carry

    lax.fori_loop(0, CH, forward_steps, 0)
    grad_core()

    def adjoint_steps(ch, carry):
        adjoint(ch)

        @pl.when(ch == 0)
        def _():
            exchange(3, s4, r4, 0)
            grad_line()

        @pl.when(ch == 1)
        def _():
            grad_row()

        @pl.when(ch == 2)
        def _():
            grad_column()

        return carry

    lax.fori_loop(0, CH, adjoint_steps, 0)

    for b in range(8):
        pps[b, 0:16, :] = dwe[b * 16 : b * 16 + 16, :]
        pps[b, 16:32, :] = db[...]
    to_plane(lambda other: pps.at[other], ppr.at[bme], 7)
    exchange(3, s4, r4, 1)

    def last_line():
        drain(ppr.at[pl.ds(0, 7)], gr.at[7])
        total = pps[bme]
        for step in range(1, 8):
            total = total + ppr[lax.rem(bme + step, 8)]
        px[0:32, :] = total
        square = grad_block()
        px[32:40, :] = square[0:8] + square[8:16]
        to_line(lambda other: px, pxr.at[xme], 8)

    def last_column():
        drain(pxr.at[pl.ds(0, 3)], gr.at[8])
        total = px[...]
        for step in range(1, XS):
            total = total + pxr[lax.rem(xme + step, XS)]
        pzl[...] = total[0:16].astype(bf16)
        pz[...] = jnp.zeros((8, 128), f32)
        two_rows = jnp.zeros((2, 128), f32)
        for k in range(8):
            chosen = jnp.where(bme == k, 1.0, 0.0)
            two_rows = two_rows + chosen * total[16 + 2 * k : 18 + 2 * k]
        pz[0:2, :] = two_rows
        pz[2:3, :] = jnp.sum(total[32:40], axis=0, keepdims=True)
        to_column(pz, pzr.at[zme], 9)
        to_column(pzl, pzlr.at[zme], 13)

    def last_plane():
        drain(pzr.at[pl.ds(0, 7)], gr.at[9])
        drain(pzlr.at[pl.ds(0, 7)], gr.at[13])
        total = pz[...]
        wide_total = pzl[...].astype(f32)
        for step in range(1, 8):
            total = total + pzr[lax.rem(zme + step, 8)]
            wide_total = wide_total + pzlr[lax.rem(zme + step, 8)].astype(f32)
        tot[0:16, :] = wide_total
        tot[16:24, :] = total
        pgr[bme] = tot[...]
        to_plane(lambda other: tot, pgr.at[bme], 10)


    def finish(ch, carry):
        arrived(3, r4, ch)
        for row in range(2):
            grid = dot(bi[row], unpack(r4[ch], row))
            gv[2 * ch, row] = grid[:, 0:128]
            gv[2 * ch + 1, row] = grid[:, 128:256]

        @pl.when(ch == 0)
        def _():
            exchange(3, s4, r4, 2)
            last_line()
            last_column()

        @pl.when(ch == 1)
        def _():
            exchange(3, s4, r4, 3)

        @pl.when(ch == 2)
        def _():
            last_plane()

        return carry

    lax.fori_loop(0, CH, finish, 0)

    drain(pgr.at[pl.ds(0, 7)], gr.at[10])
    enc = pgr[:, 0:16, :].reshape(128, 128)
    row = lax.broadcasted_iota(jnp.int32, (128, 128), 0)
    first_row = 640 * xme + 10 * me
    wide[0:128, :] = jnp.where((row >= first_row) & (row < first_row + 10), enc, 0.0)
    wide[128:160, :] = jnp.zeros((32, 128), f32)

    @pl.when((xme == 0) & (zme < 2))
    def _():
        begin = pl.multiple_of(80 * zme + 8 * lax.div(10 * bme, 8), 8)
        blk[...] += wide[pl.ds(begin, 16), :]

    for b in range(8):
        fin[2 * b : 2 * b + 2, :] = pgr[b, 16:18, :]
    bias_total = fin[0:16, :]
    squares = (
        jnp.sum(pgr[:, 18, :]) + jnp.sum(enc * enc) + jnp.sum(bias_total * bias_total)
    )
    norm = jnp.sqrt(jnp.zeros((8, 128), f32) + squares)
    clip = jnp.minimum(1.0, clip_norm / (norm + 1e-06))
    both_clip = jnp.concatenate([clip, clip], axis=0)
    fin[0:16, :] = bias_total * both_clip
    fin[16:24, :] = norm
    blk[...] = blk[...] * both_clip

    for phase, src in enumerate((s1, s2, s3, s4)):
        for ch in range(CH):
            drain(src.at[ch, pl.ds(0, LATS - 1)], ssem.at[phase, ch])
    drain(wz.at[pl.ds(0, 7)], gs.at[0])
    drain(wb.at[0, pl.ds(0, 7)], gs.at[1])
    drain(wb.at[pl.ds(0, 3), pl.ds(0, 4)], gs.at[2])
    drain(wb.at[pl.ds(0, 3), pl.ds(0, 4)], gs.at[11])
    drain(rk, gs.at[12])
    drain(rx.at[pl.ds(0, 3)], gs.at[3])
    drain(ry.at[pl.ds(0, 3)], gs.at[4])

    turn_bytes(gs.at[5])
    drain(ppr.at[pl.ds(0, 7)], gs.at[7])
    drain(pxr.at[pl.ds(0, 3)], gs.at[8])
    drain(pzr.at[pl.ds(0, 7)], gs.at[9])
    drain(pzlr.at[pl.ds(0, 7)], gs.at[13])
    drain(pgr.at[pl.ds(0, 7)], gs.at[10])


def adam_update(weights, moment, second, grads, lost_one, lost_two):
    moment_new = beta_one * moment + (1.0 - beta_one) * grads
    second_new = beta_two * second + (1.0 - beta_two) * grads * grads
    moment_hat = moment_new / lost_one
    second_hat = second_new / lost_two
    weights_new = weights - learn_rate * (
        moment_hat / (jnp.sqrt(second_hat) + adam_eps) + decay_rate * weights
    )
    return (weights_new, moment_new, second_new)


def update_kernel(
    so_in,
    sg_in,
    blk,
    fin,
    mat,
    mat_m,
    mat_s,
    bias,
    bias_m,
    bias_s,
    steps,
    so_out,
    sg_out,
    mat_grad,
    mat_new,
    mat_copy,
    mat_m_new,
    mat_s_new,
    bias_grad,
    bias_new,
    bias_m_new,
    bias_s_new,
    norm,
    mat_grad_v,
    mat_new_v,
    mat_copy_v,
    mat_m_new_v,
    mat_s_new_v,
    bias_grad_v,
    bias_new_v,
    bias_m_new_v,
    bias_s_new_v,
    norm_v,
    sems,
):
    def piece(number):
        which, part = number % 2, pl.ds(2 * (number // 2), 2)
        return pltpu.make_async_copy(
            (so_in, sg_in)[which].at[part], (so_out, sg_out)[which].at[part], sems.at[number]
        )

    for number in range(2 * CH):
        piece(number).start()
    count = jnp.broadcast_to(steps[...].astype(f32), (1, 128))
    lost_one = 1.0 - jnp.exp(count * math.log(beta_one))
    lost_two = 1.0 - jnp.exp(count * math.log(beta_two))
    block = blk[...]
    place = 2 * lax.rem(lax.axis_index("lat"), 4)
    grads = jnp.zeros((10, 128), f32)
    for begin in (0, 2, 4, 6):
        grads = jnp.where(place == begin, block[begin : begin + 10], grads)
    mat_grad_v[...] = grads
    new, moment, second = adam_update(mat[...], mat_m[...], mat_s[...], grads, lost_one, lost_two)
    mat_new_v[...] = new
    mat_copy_v[...] = new.astype(bf16)
    mat_m_new_v[...] = moment
    mat_s_new_v[...] = second
    grads = fin[0:BIAS_ROWS, :]
    bias_grad_v[...] = grads
    new, moment, second = adam_update(
        bias[...], bias_m[...], bias_s[...], grads, lost_one, lost_two
    )
    bias_new_v[...] = new
    bias_m_new_v[...] = moment
    bias_s_new_v[...] = second
    norm_v[...] = fin[16:17, 0:1]
    small = [
        pltpu.make_async_copy(mat_grad_v, mat_grad, sems.at[8]),
        pltpu.make_async_copy(mat_new_v, mat_new, sems.at[9]),
        pltpu.make_async_copy(mat_copy_v, mat_copy, sems.at[10]),
        pltpu.make_async_copy(mat_m_new_v, mat_m_new, sems.at[11]),
        pltpu.make_async_copy(mat_s_new_v, mat_s_new, sems.at[12]),
        pltpu.make_async_copy(bias_grad_v, bias_grad, sems.at[13]),
        pltpu.make_async_copy(bias_new_v, bias_new, sems.at[14]),
        pltpu.make_async_copy(bias_m_new_v, bias_m_new, sems.at[15]),
        pltpu.make_async_copy(bias_s_new_v, bias_s_new, sems.at[16]),
        pltpu.make_async_copy(norm_v, norm, sems.at[17]),
    ]
    for copy in small:
        copy.start()
    for number in range(2 * CH):
        piece(number).wait()
    for copy in small:
        copy.wait()


def local(
    state,
    forcing,
    state_cot,
    mat_master,
    mat_moment,
    mat_second,
    bias_master,
    bias_moment,
    bias_second,
    level_coupling,
    lat_of_row,
    step_count,
):
    both, turned = zonal_tables()
    any_spec = pl.BlockSpec(memory_space=pl.ANY)
    big = (8, 2, NLON, C)
    tiles = (CH, LATS, 16, 128)
    vm = pltpu.VMEM
    scratch = [
        vm(big, f32),
        vm(big, bf16),
        vm(big, f32),
        vm((10, 128), f32),
        vm((16, 128), bf16),
        vm((BIAS_ROWS, 128), f32),
        vm((1, 128), jnp.int32),
        vm((128, 128), f32),
        vm((2, 256, 256), bf16),
        vm((2, 256, 256), bf16),
        *[vm(tiles, bf16) for _ in range(8)],
        *[vm((2, 128, 128), bf16) for _ in range(4)],
        vm((1040, 128), f32),
        vm((CH, 1024, 128), bf16),
        vm((2, 128, 128), f32),
        vm((2, 2, 128, 128), f32),
        vm((2, 128, 128), f32),
        vm((2, 128, 128), f32),
        vm((128, 128), f32),
        vm((8, 16, 128), bf16),
        vm((80, 128), f32),
        vm((XS, 8, 80, 128), bf16),
        vm((2560, 128), f32),
        vm((128, 128), bf16),
        vm((4, 256, 256), bf16),
        vm((256, 128), bf16),
        vm((128, 128), bf16),
        vm((2, 128, 128), bf16),
        vm((2, 256, 256), f32),
        vm((5, 512, 256), bf16),
        vm((4, 512, 256), f32),
        vm((128, 128), f32),
        vm((4, 256, 256), f32),
        vm((256, 128), f32),
        vm((128, 128), f32),
        vm((16, 128), f32),
        vm((2560, 128), f32),
        vm((16, 80, 128), f32),
        vm((16, 80, 128), bf16),
        vm((XS, 4, 80, 128), bf16),
        vm((4, 80, 128), f32),
        vm((4, 80, 128), f32),
        vm((8, 16, 128), bf16),
        vm((8, 16, 128), bf16),
        vm((160, 128), f32),
        vm((8, 32, 128), f32),
        vm((8, 32, 128), f32),
        vm((40, 128), f32),
        vm((XS, 40, 128), f32),
        vm((8, 128), f32),
        vm((8, 8, 128), f32),
        vm((16, 128), bf16),
        vm((8, 16, 128), bf16),
        vm((24, 128), f32),
        vm((8, 24, 128), f32),
        pltpu.SemaphoreType.DMA((CH,)),
        pltpu.SemaphoreType.DMA((10,)),
        pltpu.SemaphoreType.DMA((4, CH)),
        pltpu.SemaphoreType.DMA((4, CH)),
        pltpu.SemaphoreType.DMA((14,)),
        pltpu.SemaphoreType.DMA((14,)),
    ]
    vm_spec = pl.BlockSpec(memory_space=pltpu.VMEM)
    operands = (
        state,
        forcing,
        state_cot,
        mat_master.reshape(10, 128),
        bias_master.reshape(BIAS_ROWS, 128),
        lat_of_row.reshape(1, 128),
        level_coupling,
        jnp.asarray(both),
        jnp.asarray(turned),
    )
    held = pl.pallas_call(
        kernel,
        out_shape=(vm(big, f32), vm(big, f32), vm((16, 128), f32), vm((24, 128), f32)),
        in_specs=[any_spec] * 9,
        out_specs=(vm_spec,) * 4,
        scratch_shapes=scratch,
        compiler_params=pltpu.CompilerParams(
            collective_id=0, has_side_effects=True, vmem_limit_bytes=56 * 1024 * 1024
        ),
        cost_estimate=pl.CostEstimate(
            flops=16 * 10**9, bytes_accessed=10 * 2**20, transcendentals=4 * 10**6
        ),
        name="column_step",
    )(*[pltpu.with_memory_space_constraint(part, pltpu.HBM) for part in operands])

    mat_shape = jax.ShapeDtypeStruct((10, 128), f32)
    bias_shape = jax.ShapeDtypeStruct((BIAS_ROWS, 128), f32)
    results = pl.pallas_call(
        update_kernel,
        out_shape=(
            jax.ShapeDtypeStruct(big, f32),
            jax.ShapeDtypeStruct(big, f32),
            mat_shape,
            mat_shape,
            jax.ShapeDtypeStruct((10, 128), bf16),
            mat_shape,
            mat_shape,
            bias_shape,
            bias_shape,
            bias_shape,
            bias_shape,
            jax.ShapeDtypeStruct((1, 1), f32),
        ),
        in_specs=[vm_spec] * 11,
        out_specs=(any_spec,) * 12,
        scratch_shapes=[
            *[vm((10, 128), f32), vm((10, 128), f32), vm((10, 128), bf16)],
            *[vm((10, 128), f32) for _ in range(2)],
            *[vm((BIAS_ROWS, 128), f32) for _ in range(4)],
            vm((1, 1), f32),
            pltpu.SemaphoreType.DMA((2 * CH + 10,)),
        ],
        compiler_params=pltpu.CompilerParams(vmem_limit_bytes=16 * 1024 * 1024),
        cost_estimate=pl.CostEstimate(flops=10**5, bytes_accessed=8 * 2**20, transcendentals=10**4),
        name="weight_step",
    )(
        *[pltpu.with_memory_space_constraint(part, pltpu.VMEM) for part in held],
        mat_master.reshape(10, 128),
        mat_moment.reshape(10, 128),
        mat_second.reshape(10, 128),
        bias_master.reshape(BIAS_ROWS, 128),
        bias_moment.reshape(BIAS_ROWS, 128),
        bias_second.reshape(BIAS_ROWS, 128),
        step_count.reshape(1, 1),
    )
    return results[0:2] + tuple(part.reshape(-1) for part in results[2:])


def solution(mesh):
    columns = P("dp", "lat", None, None)
    flat = P(("dp", "lat"))
    return jax.shard_map(
        local,
        mesh=mesh,
        in_specs=(columns,) * 3 + (flat,) * 3 + (P(),) * 6,
        out_specs=(columns,) * 2 + (flat,) * 5 + (P(),) * 5,
        check_vma=False,
    )
```
